256 devices in a mesh: space: 32 (over x, z_lo, core), tm: 8 (over z_hi, y).
Axes of the slice: x: 4, y: 4, z: 8 (z_hi: 2, z_lo: 4; z = z_hi * 4 + z_lo), core: 2. Of those that a mesh axis runs over, the one named last changes fastest.
Arguments:
- node_feats: bfloat16 [128, 14336, 128], P('tm', 'space'), may hold values from -6 to 6
- positions: float32 [128, 3, 14336], P('tm', None, 'space'), may hold values from -3 to 3
- neighbours: int32 [128, 448, 8], P('tm', 'space'), may hold values from 0 to 447, as said below
- edge_in: bfloat16 [256, 128], replicated, may hold values from -0.375 to 0.375
- edge_out: bfloat16 [128, 128], replicated, may hold values from -0.5 to 0.5
- edge_params: float32 [3, 128], replicated, may hold values from -3 to 3
- coord_weight: float32 [128], replicated, may hold values from -0.5 to 0.5
- spectral: bfloat16 [2, 64, 128, 128], replicated, may hold values from -0.375 to 0.375
- node_in: bfloat16 [256, 128], replicated, may hold values from -0.375 to 0.375
- node_out: bfloat16 [128, 128], replicated, may hold values from -0.5 to 0.5
- node_bias: float32 [2, 128], replicated, may hold values from -3 to 3
Outputs:
- new_feats: bfloat16 [128, 14336, 128], P('tm', 'space')
- new_positions: float32 [128, 3, 14336], P('tm', None, 'space')
The draws below stay inside these ranges and needn't reach their ends.
Inputs may be any that keep to these rules, and one draw needn't show every extreme that they name: neighbours[f, b, s] = (b + o) mod 448 for an offset o with -6 <= o <= 6; the offsets of a block's list may repeat, and every list holds the offsets 0, -6 and +6 in some slots.
All inputs are finite; a program needn't handle non-finite values.
Results may differ from the reference program's by a relative error of at most 0.0065.
Values may be sent and summed in bfloat16 or wider, within the bound.
A program may use at most 128 MiB of HBM per device.

```python
import jax
import jax.numpy as jnp
from jax import lax

H = 128
FRAMES = 128
MODES = 64
NBR = 8
BLOCK = 32
GHOST = 6
P_DEV = 448
PARTICLES = 14336
NBLOCKS = 448


def draw_neighbours(key, part):
    offset_key, order_key = jax.random.split(jax.random.fold_in(key, 17))
    extra_slots = jax.random.randint(offset_key, (FRAMES, NBLOCKS, NBR - 3), -GHOST, GHOST + 1, dtype=jnp.int32)
    fixed_slots = jnp.broadcast_to(jnp.array([0, -GHOST, GHOST], dtype=jnp.int32), (FRAMES, NBLOCKS, 3))
    offsets = jnp.concatenate([fixed_slots, extra_slots], axis=-1)
    scores = jax.random.randint(order_key, (FRAMES, NBLOCKS, NBR), 0, 1 << 20, dtype=jnp.int32) * NBR + jnp.arange(NBR, dtype=jnp.int32)
    ordering = jnp.argsort(scores, axis=-1)
    offsets = jnp.take_along_axis(offsets, ordering, axis=-1)
    block_ids = jnp.arange(NBLOCKS, dtype=jnp.int32)[None, :, None]
    return ((block_ids + offsets) % NBLOCKS).astype(jnp.int32)


def block_scale(own_key, extent, cuts, low, high):
    def one(position, blocks):
        steps = jax.random.uniform(jax.random.fold_in(jax.random.fold_in(own_key, 6), position), (blocks,), jnp.float32, low / len(cuts), high / len(cuts))
        return jnp.repeat(jnp.exp(steps), extent[position] // blocks).reshape((-1,) + (1,) * (len(extent) - position - 1))

    gain = one(*cuts[0])
    for cut in cuts[1:]:
        gain = gain * one(*cut)
    return gain


def gaussian(stream_key, dims, deviation, limit, shards=(), kind=jnp.bfloat16):
    result = deviation * jax.random.normal(stream_key, dims, jnp.float32)
    if shards:
        result = result * block_scale(stream_key, dims, shards, -0.22, 0.18)
    return jnp.clip(result, -limit, limit).astype(kind)


def setup_inputs(seed: int = 0) -> dict:
    seeds = jax.random.split(jax.random.key(seed), 12)
    node_feats = gaussian(seeds[0], (FRAMES, PARTICLES, H), 1.0, 6.0, ((0, 8), (1, 32)))
    positions = gaussian(seeds[1], (FRAMES, 3, PARTICLES), 0.5, 3.0, ((0, 8), (2, 32)), jnp.float32)
    neighbours = draw_neighbours(jax.random.fold_in(seeds[11], 71), 0)
    edge_in = gaussian(seeds[3], (2 * H, H), (2 * H) ** -0.5, 0.375)
    edge_out = gaussian(seeds[4], (H, H), H ** -0.5, 0.5)
    edge_params = gaussian(seeds[5], (3, H), 0.5, 3.0, (), jnp.float32)
    coord_weight = gaussian(seeds[6], (H,), H ** -0.5, 0.5, (), jnp.float32)
    spectral = gaussian(seeds[7], (2, MODES, H, H), (2 * H) ** -0.5, 0.375)
    node_in = gaussian(seeds[8], (2 * H, H), (2 * H) ** -0.5, 0.375)
    node_out = gaussian(seeds[9], (H, H), H ** -0.5, 0.5)
    node_bias = gaussian(seeds[10], (2, H), 0.5, 3.0, (), jnp.float32)
    return dict(node_feats=node_feats, positions=positions, neighbours=neighbours, edge_in=edge_in, edge_out=edge_out, edge_params=edge_params, coord_weight=coord_weight, spectral=spectral, node_in=node_in, node_out=node_out, node_bias=node_bias)


def frame_edges(frame_feats, frame_pos, frame_nbr, edge_in, edge_out, edge_params, coord_weight):
    feat_width = frame_feats.shape[1]
    block_count = frame_nbr.shape[0]
    own_src = jnp.dot(frame_feats, edge_in[:feat_width], preferred_element_type=jnp.float32).reshape(block_count, BLOCK, feat_width)
    all_dst = jnp.dot(frame_feats, edge_in[feat_width:], preferred_element_type=jnp.float32).reshape(block_count, BLOCK, feat_width)
    own_pos = frame_pos.reshape(3, block_count, BLOCK)
    summed = jnp.zeros(own_src.shape, jnp.float32)
    moved = jnp.zeros(own_pos.shape, jnp.float32)
    for slot_num in range(NBR):
        chosen = frame_nbr[:, slot_num]
        near_dst = all_dst[chosen]
        near_pos = own_pos[:, chosen]
        offset_vec = own_pos - near_pos
        dist_sq = lax.optimization_barrier(jnp.sum(offset_vec * offset_vec, axis=0))
        pre_act = own_src + near_dst + edge_params[0] + dist_sq[:, :, None] * edge_params[1]
        hidden = jax.nn.silu(pre_act).astype(jnp.bfloat16)
        out_act = jnp.dot(hidden.reshape(-1, feat_width), edge_out, preferred_element_type=jnp.float32).reshape(pre_act.shape) + edge_params[2]
        message = jax.nn.silu(out_act)
        summed = summed + message
        weight = lax.optimization_barrier(jnp.sum(message * coord_weight, axis=-1)) / (1.0 + jnp.sqrt(dist_sq + 1.0))
        moved = moved + offset_vec * weight[None]
    mean_msg = (summed / NBR).astype(jnp.bfloat16).reshape(-1, feat_width)
    new_pos = frame_pos + (moved / NBR).reshape(3, -1)
    return (mean_msg, new_pos)

def spectral_piece(msg_block, spectral):
    spectrum = jnp.fft.rfft(msg_block.astype(jnp.float32), axis=0)[:MODES]
    real_c = spectrum.real.astype(jnp.bfloat16)
    imag_c = spectrum.imag.astype(jnp.bfloat16)
    real_c, imag_c = lax.optimization_barrier((real_c, imag_c))
    real_c = real_c.astype(jnp.float32)
    imag_c = imag_c.astype(jnp.float32)
    real_w = spectral[0].astype(jnp.float32)
    imag_w = spectral[1].astype(jnp.float32)
    mixed_real = jnp.einsum('knh,khg->kng', real_c, real_w) - jnp.einsum('knh,khg->kng', imag_c, imag_w)
    mixed_imag = jnp.einsum('knh,khg->kng', real_c, imag_w) + jnp.einsum('knh,khg->kng', imag_c, real_w)
    upper = jnp.zeros((FRAMES // 2 + 1 - MODES,) + mixed_real.shape[1:], mixed_real.dtype)
    full_spec = jnp.concatenate([mixed_real, upper], axis=0) + 1j * jnp.concatenate([mixed_imag, upper], axis=0)
    return jnp.fft.irfft(full_spec, n=FRAMES, axis=0).astype(jnp.bfloat16)

def node_update(frame_feats, frame_conv, node_in, node_out, node_bias):
    feat_width = frame_feats.shape[1]
    pre_act = jnp.dot(frame_feats, node_in[:feat_width], preferred_element_type=jnp.float32) + jnp.dot(frame_conv, node_in[feat_width:], preferred_element_type=jnp.float32) + node_bias[0]
    hidden = jax.nn.silu(pre_act).astype(jnp.bfloat16)
    return (frame_feats.astype(jnp.float32) + (jnp.dot(hidden, node_out, preferred_element_type=jnp.float32) + node_bias[1])).astype(jnp.bfloat16)

def reference(node_feats, positions, neighbours, edge_in, edge_out, edge_params, coord_weight, spectral, node_in, node_out, node_bias):

    def per_frame(inputs):
        return frame_edges(inputs[0], inputs[1], inputs[2], edge_in, edge_out, edge_params, coord_weight)
    mean_msg, new_positions = lax.map(per_frame, (node_feats, positions, neighbours))
    piece_count = mean_msg.shape[1] // P_DEV

    def one_piece(piece_num):
        piece = lax.dynamic_slice_in_dim(mean_msg, piece_num * P_DEV, P_DEV, 1)
        return spectral_piece(piece, spectral)
    stacked = lax.map(one_piece, jnp.arange(piece_count, dtype=jnp.int32))
    conv_all = jnp.transpose(stacked, (1, 0, 2, 3)).reshape(FRAMES, -1, mean_msg.shape[2])

    def per_node(inputs):
        return node_update(inputs[0], inputs[1], node_in, node_out, node_bias)
    new_feats = lax.map(per_node, (node_feats, conv_all))
    return (new_feats, new_positions)
```

```python
import math

import jax
import jax.numpy as jnp
import numpy as np
from jax import lax
from jax.experimental import pallas as pl
from jax.experimental.pallas import tpu as pltpu
from jax.sharding import PartitionSpec as P

H = 128
L = 32
G = 6
FR = 16
NB = 14
EXT = NB + 2 * G
S = 8
T = 128
K = 64
PAIRS = 7
LAG = 2
MESH = pl.DeviceIdType.MESH
F32 = jnp.float32
BF = jnp.bfloat16


def dot(a, b):
    return jnp.dot(a, b, preferred_element_type=F32)


def split_np(values):
    import ml_dtypes

    high = values.astype(ml_dtypes.bfloat16)
    low = (values - high.astype(np.float64)).astype(ml_dtypes.bfloat16)
    return high, low


def transforms():
    k = np.arange(K)
    t = np.arange(T)
    angle = 2.0 * math.pi / T * ((k[:, None] * t[None, :]) % T)
    forward = np.concatenate([np.cos(angle), -np.sin(angle)], axis=0)
    fwd = np.concatenate(split_np(forward), axis=0)
    weight = (np.where(k == 0, 1.0, 2.0) / T)[None, :]
    inverse = np.concatenate([np.cos(angle.T) * weight, -np.sin(angle.T) * weight], axis=1)
    inv_hi, inv_lo = split_np(inverse)
    return jnp.asarray(fwd), jnp.asarray(inv_hi), jnp.asarray(inv_lo)


def rows(start, size):
    return pl.ds(pl.multiple_of(start, size), size)


def kernel(
    idx,
    pos3,
    edge_in,
    edge_out,
    edge_params,
    coord_w,
    node_in,
    node_out,
    node_bias,
    fwd,
    inv_hi,
    inv_lo,
    feats_hbm,
    spec_hbm,
    out,
    out_pos,
    ext,
    ghost,
    pt,
    po,
    near,
    scaled,
    acc_buf,
    send_buf,
    recv_buf,
    conv_buf,
    back_buf,
    spec,
    coef,
    mixed,
    node_buf,
    w_src,
    w_dst,
    w_edge,
    w_coord,
    w_n1,
    w_n2,
    loc_sem,
    pos_send,
    pos_recv,
    halo_send,
    halo_recv,
    msg_send,
    msg_recv,
    conv_send,
    conv_recv,
):
    sp = lax.axis_index("space")
    tm = lax.axis_index("tm")
    count = lax.axis_size("space")
    y = tm % 4
    half = tm // 4
    right = (sp + 1) % count
    left = (sp + count - 1) % count

    def partner_y(d):
        if d % 4 == 0:
            return y
        if d % 4 == 1:
            return y + 1 - 2 * (y % 2)
        if d % 4 == 2:
            return (y + 2) % 4
        return 3 - y

    def partner(d):
        return (1 - half if d >= 4 else half) * 4 + partner_y(d)

    barrier = pltpu.get_barrier_semaphore()
    for other in (left, right):
        pl.semaphore_signal(barrier, inc=1, device_id=(other, tm), device_id_type=MESH)
    for d in range(1, 8):
        pl.semaphore_signal(barrier, inc=1, device_id=(sp, partner(d)), device_id_type=MESH)

    own_copy = pltpu.make_async_copy(feats_hbm, ext.at[:, pl.ds(G, NB)], loc_sem.at[0])
    own_copy.start()
    spec_copy = pltpu.make_async_copy(spec_hbm, spec, loc_sem.at[1])
    spec_copy.start()

    group16 = lax.broadcasted_iota(jnp.int32, (FR, 128), 1) // L
    for b in range(NB):
        q, w = b // 4, b % 4
        tile = jnp.zeros((FR, 128), F32)
        for d in range(3):
            part = pos3[d, :, q * 128 : (q + 1) * 128]
            shift = (L * (d - w)) % 128
            if shift:
                part = pltpu.roll(part, shift, 1)
            tile = jnp.where(group16 == d, part, tile)
        pt[G + b] = tile

    pl.semaphore_wait(barrier, 9)

    def pos_copy(side):
        if side == 0:
            src, dst, dev = NB, 0, right
        else:
            src, dst, dev = G, G + NB, left
        return pltpu.make_async_remote_copy(
            src_ref=pt.at[pl.ds(src, G)],
            dst_ref=pt.at[pl.ds(dst, G)],
            send_sem=pos_send.at[side],
            recv_sem=pos_recv.at[side],
            device_id=(dev, tm),
            device_id_type=MESH,
        )

    def halo_copy(side, q):
        if side == 0:
            src, dev = NB - 1 - q, right
        else:
            src, dev = q, left
        return pltpu.make_async_remote_copy(
            src_ref=feats_hbm.at[:, src],
            dst_ref=ghost.at[side, q],
            send_sem=halo_send.at[side, q],
            recv_sem=halo_recv.at[side, q],
            device_id=(dev, tm),
            device_id_type=MESH,
        )

    def msg_copy(j, d):
        return pltpu.make_async_remote_copy(
            src_ref=send_buf.at[j, :, rows(partner_y(d) * 8, 8)],
            dst_ref=recv_buf.at[j, :, :, rows(tm * FR, FR), :],
            send_sem=msg_send.at[j, d - 1],
            recv_sem=msg_recv.at[j, d - 1],
            device_id=(sp, partner(d)),
            device_id_type=MESH,
        )

    def conv_copy(j, d):
        return pltpu.make_async_remote_copy(
            src_ref=conv_buf.at[j, :, :, rows(partner_y(d) * FR, FR), :],
            dst_ref=back_buf.at[j, :, y],
            send_sem=conv_send.at[j, d - 1],
            recv_sem=conv_recv.at[j, d - 1],
            device_id=(sp, partner(d)),
            device_id_type=MESH,
        )

    for side in range(2):
        pos_copy(side).start()
    for q in range(G):
        for side in range(2):
            halo_copy(side, q).start()

    def half_bf(v):
        return (v.astype(F32) * 0.5).astype(BF)

    zero = jnp.zeros((H, H), BF)
    src_half = half_bf(edge_in[:H, :])
    dst_half = half_bf(edge_in[H:, :])
    edge_half = half_bf(edge_out[...])
    row = lax.broadcasted_iota(jnp.int32, (H, H), 0)
    lane = lax.broadcasted_iota(jnp.int32, (H, H), 1)
    bias = edge_params[0:1, :] * 0.5
    dist_w = edge_params[1:2, :] * 0.5

    def split3(v):
        a = v.astype(BF).astype(F32)
        r = v - a
        b = r.astype(BF).astype(F32)
        return a, b, (r - b).astype(BF).astype(F32)

    bias_parts = split3(bias)
    dist_hi, dist_lo, _ = split3(dist_w)
    cw_hi = jnp.broadcast_to(coord_w[...], (H, H)).T
    cw_hi, cw_lo, _ = split3(cw_hi)
    for s in range(S):
        p, c = s // 2, (s % 2) * H
        w_src[p, :H, c : c + H] = src_half
        block = jnp.where((row == s) | (row == 8 + s), dist_hi, 0.0)
        block = jnp.where(row == 16 + s, dist_lo, block)
        for i in range(3):
            block = jnp.where(row == 24 + i, bias_parts[i], block)
        w_src[p, H:, c : c + H] = block.astype(BF)
        w_coord[p, c : c + H, :] = jnp.where(
            lane == s, cw_hi, jnp.where(lane == 8 + s, cw_lo, 0.0)
        ).astype(BF)
    for dst_ref, w in ((w_dst, dst_half), (w_edge, edge_half)):
        dst_ref[:H, :H] = w
        dst_ref[H:, H:] = w
        dst_ref[:H, H:] = zero
        dst_ref[H:, :H] = zero
    w_n1[...] = half_bf(node_in[:H, :])
    w_n2[...] = half_bf(node_in[H:, :])
    edge_bias = edge_params[2:3, :] * 0.5
    edge_bias2 = jnp.concatenate([edge_bias, edge_bias], axis=1)
    node_b0 = node_bias[0:1, :] * 0.5
    node_b1 = node_bias[1:2, :]

    for side in range(2):
        pos_copy(side).wait()
    own_copy.wait()

    group = lax.broadcasted_iota(jnp.int32, (8, 128), 1) // L

    def own_rows(f, b):
        return ext[f, G + b]

    def edge_block(j, e, b):
        def frame_group(fg, carry):
            dist = jnp.zeros((8, 128), F32)
            for u in range(4):
                f = fg * 4 + u
                base = (f * NB + b) * S
                for s in range(S):
                    near[u * 8 + s : u * 8 + s + 1, :] = pt[idx[base + s], pl.ds(f, 1), :]
                own = pt[G + b, pl.ds(f, 1), :]
                offset = own - near[u * 8 : (u + 1) * 8, :]
                square = offset * offset
                square = square + pltpu.roll(square, 64, 1)
                square = square + pltpu.roll(square, 32, 1)
                scaled[u * 8 : (u + 1) * 8, :] = offset / (1.0 + jnp.sqrt(square + 1.0))
                dist = jnp.where(group == u, square, dist)
            d_hi = dist.astype(BF).astype(F32)
            d_lo = (dist - d_hi).astype(BF).astype(F32)
            aug = jnp.concatenate(
                [d_hi, d_lo, d_hi, jnp.ones((8, 128), F32), jnp.zeros((96, 128), F32)], axis=0
            )
            aug = aug.T.astype(BF)
            own_f = jnp.concatenate([own_rows(fg * 4 + u, b) for u in range(4)], axis=0)
            first = jnp.concatenate([own_f, aug], axis=1)
            acc = jnp.zeros((H, H), F32)
            wsum = jnp.zeros((H, H), F32)
            for p in range(4):
                cols = []
                for s in (2 * p, 2 * p + 1):
                    parts = []
                    for u in range(4):
                        f = fg * 4 + u
                        i = idx[(f * NB + b) * S + s]
                        parts.append(ext[f, i])
                    cols.append(jnp.concatenate(parts, axis=0))
                second = jnp.concatenate(cols, axis=1)
                pre = dot(first, w_src[p]) + dot(second, w_dst[...])
                hidden = (pre * jnp.tanh(pre) + pre).astype(BF)
                act = dot(hidden, w_edge[...]) + edge_bias2
                msg = act * jnp.tanh(act) + act
                acc = acc + (msg[:, :H] + msg[:, H:])
                wsum = wsum + dot(msg.astype(BF), w_coord[p])
            acc_buf[rows(fg * 128, 128), :] = acc * (1.0 / S)
            wt = wsum.T
            wv = wt[0:8, :] + wt[8:16, :]
            for u in range(4):
                f = fg * 4 + u
                one = jnp.where(group == u, wv, 0.0)
                one = one + pltpu.roll(one, 64, 1)
                one = one + pltpu.roll(one, 32, 1)
                moved = jnp.sum(scaled[u * 8 : (u + 1) * 8, :] * one, axis=0, keepdims=True)
                own = pt[G + b, pl.ds(f, 1), :]
                po[pl.ds(b * FR + f, 1), :] = own + moved * (1.0 / S)
            return carry

        lax.fori_loop(0, 4, frame_group, 0)
        for l in range(L):
            send_buf[j, e, l] = acc_buf[pl.ds(l, FR, stride=L), :].astype(BF)
        recv_buf[j, e, :, rows(tm * FR, FR), :] = send_buf[j, e, rows(y * 8, 8)]

    def edge_pair(j):
        @pl.when(j >= 1)
        def _():
            q = j - 1
            for side in range(2):
                halo_copy(side, q).wait_recv()
            for f in range(FR):
                ext[f, G - 1 - q] = ghost[0, q, f]
                ext[f, G + NB + q] = ghost[1, q, f]

        edge_block(j, 0, 6 - j)
        edge_block(j, 1, 7 + j)
        for d in (4, 5, 7, 6, 1, 3, 2):
            msg_copy(j, d).start()

    def spectral_pair(j):
        for d in range(1, 8):
            msg_copy(j, d).wait_recv()
        for e in range(2):

            def analyse(r, carry):
                c2 = dot(fwd[...], recv_buf[j, e, r])
                coef[rows((e * 8 + r) * T, T), :] = c2[:T] + c2[T:]
                return carry

            lax.fori_loop(0, 8, analyse, 0)

        def mode(k, carry):
            re = coef[pl.ds(k, 16, stride=T), :].astype(BF)
            im = coef[pl.ds(K + k, 16, stride=T), :].astype(BF)
            lhs = jnp.concatenate(
                [jnp.concatenate([re, -im], axis=1), jnp.concatenate([im, re], axis=1)], axis=0
            )
            w = jnp.concatenate([spec[0, k], spec[1, k]], axis=0)
            m = dot(lhs, w)
            mixed[rows(k * 16, 16), :] = m[:16]
            mixed[rows((K + k) * 16, 16), :] = m[16:]
            return carry

        lax.fori_loop(0, K, mode, 0)
        rows_t = rows(half * 64, 64)
        for e in range(2):

            def synth(r, carry):
                m = mixed[pl.ds(e * 8 + r, T, stride=16), :]
                hi = m.astype(BF)
                lo = (m - hi.astype(F32)).astype(BF)
                ihi = inv_hi[rows_t, :]
                c = dot(ihi, hi) + dot(inv_lo[rows_t, :], hi) + dot(ihi, lo)
                conv_buf[j, e, r] = c.astype(BF)
                return carry

            lax.fori_loop(0, 8, synth, 0)
        for d in (1, 3, 2):
            conv_copy(j, d).start()
        for e in range(2):
            back_buf[j, e, y] = conv_buf[j, e, :, rows(y * FR, FR), :]

    def node_pair(j):
        for d in (1, 3, 2):
            conv_copy(j, d).wait_recv()
        for e in range(2):
            b = 6 - j if e == 0 else 7 + j
            node_buf[...] = dot(back_buf[j, e].reshape(L * FR, H), w_n2[...])

            def frame_group(fg, carry):
                part = jnp.concatenate(
                    [node_buf[pl.ds(fg * 4 + u, L, stride=FR), :] for u in range(4)], axis=0
                )
                own = jnp.concatenate([own_rows(fg * 4 + u, b) for u in range(4)], axis=0)
                pre = dot(own, w_n1[...]) + part + node_b0
                hidden = (pre * jnp.tanh(pre) + pre).astype(BF)
                res = own.astype(F32) + (dot(hidden, node_out[...]) + node_b1)
                res = res.astype(BF)
                for u in range(4):
                    out[fg * 4 + u, rows(b * L, L), :] = res[u * L : (u + 1) * L]
                return carry

            lax.fori_loop(0, 4, frame_group, 0)

    def step(j, carry):
        @pl.when(j < PAIRS)
        def _():
            edge_pair(j)

        @pl.when(j > LAG)
        def _():
            node_pair(j - LAG - 1)

        @pl.when(j == LAG)
        def _():
            spec_copy.wait()

        @pl.when((j >= LAG) & (j < PAIRS + LAG))
        def _():
            spectral_pair(j - LAG)

        return carry

    lax.fori_loop(0, PAIRS + LAG + 1, step, 0)

    for d in range(3):
        for q in range(4):
            tile = jnp.zeros((FR, 128), F32)
            for w in range(4):
                b = q * 4 + w
                if b < NB:
                    part = po[b * FR : (b + 1) * FR, :]
                    shift = (L * (w - d)) % 128
                    if shift:
                        part = pltpu.roll(part, shift, 1)
                    tile = jnp.where(group16 == w, part, tile)
            out_pos[d, :, q * 128 : (q + 1) * 128] = tile

    for side in range(2):
        for q in range(G):
            halo_copy(side, q).wait_send()

    def drain(j, carry):
        for d in range(1, 8):
            msg_copy(j, d).wait_send()
        for d in range(1, 4):
            conv_copy(j, d).wait_send()
        return carry

    lax.fori_loop(0, PAIRS, drain, 0)


def shards(
    node_feats,
    positions,
    neighbours,
    edge_in,
    edge_out,
    edge_params,
    coord_weight,
    spectral,
    node_in,
    node_out,
    node_bias,
):
    first = lax.axis_index("space") * NB - G
    total = NB * lax.axis_size("space")
    idx = ((neighbours - first) % total).reshape(-1)
    pos3 = jnp.pad(jnp.transpose(positions, (1, 0, 2)), ((0, 0), (0, 0), (0, 64)))
    fwd, inv_hi, inv_lo = transforms()
    vmem = pl.BlockSpec(memory_space=pltpu.VMEM)
    hbm = pl.BlockSpec(memory_space=pl.ANY)
    dma = pltpu.SemaphoreType.DMA
    new_feats, pos_out = pl.pallas_call(
        kernel,
        out_shape=(
            jax.ShapeDtypeStruct((FR, NB * L, H), BF),
            jax.ShapeDtypeStruct((3, FR, 512), F32),
        ),
        in_specs=[pl.BlockSpec(memory_space=pltpu.SMEM)] + [vmem] * 11 + [hbm] * 2,
        out_specs=(vmem, vmem),
        scratch_shapes=[
            pltpu.VMEM((FR, EXT, L, H), BF),
            pltpu.VMEM((2, G, FR, L, H), BF),
            pltpu.VMEM((EXT, FR, 128), F32),
            pltpu.VMEM((NB * FR, 128), F32),
            pltpu.VMEM((32, 128), F32),
            pltpu.VMEM((32, 128), F32),
            pltpu.VMEM((FR * L, H), F32),
            pltpu.VMEM((PAIRS, 2, L, FR, H), BF),
            pltpu.VMEM((PAIRS, 2, 8, T, H), BF),
            pltpu.VMEM((PAIRS, 2, 8, 64, H), BF),
            pltpu.VMEM((PAIRS, 2, 4, 8, FR, H), BF),
            pltpu.VMEM((2, K, H, H), BF),
            pltpu.VMEM((16 * T, H), F32),
            pltpu.VMEM((16 * T, H), F32),
            pltpu.VMEM((FR * L, H), F32),
            pltpu.VMEM((4, 2 * H, 2 * H), BF),
            pltpu.VMEM((2 * H, 2 * H), BF),
            pltpu.VMEM((2 * H, 2 * H), BF),
            pltpu.VMEM((4, 2 * H, H), BF),
            pltpu.VMEM((H, H), BF),
            pltpu.VMEM((H, H), BF),
            dma((2,)),
            dma((2,)),
            dma((2,)),
            dma((2, G)),
            dma((2, G)),
            dma((PAIRS, 7)),
            dma((PAIRS, 7)),
            dma((PAIRS, 3)),
            dma((PAIRS, 3)),
        ],
        compiler_params=pltpu.CompilerParams(
            collective_id=0, has_side_effects=True, vmem_limit_bytes=56 * 1024 * 1024
        ),
    )(
        idx,
        pos3,
        edge_in,
        edge_out,
        edge_params,
        coord_weight.reshape(1, H),
        node_in,
        node_out,
        node_bias,
        fwd,
        inv_hi,
        inv_lo,
        node_feats.reshape(FR, NB, L, H),
        spectral,
    )
    new_positions = jnp.transpose(pos_out, (1, 0, 2))[:, :, : NB * L]
    return (new_feats, new_positions)


def solution(mesh):
    placed = (
        P("tm", "space", None),
        P("tm", None, "space"),
        P("tm", "space", None),
        P(),
        P(),
        P(),
        P(),
        P(),
        P(),
        P(),
        P(),
    )
    return jax.shard_map(
        shards,
        mesh=mesh,
        in_specs=placed,
        out_specs=(P("tm", "space", None), P("tm", None, "space")),
        check_vma=False,
    )
```

```python
import math

import jax
import jax.numpy as jnp
import numpy as np
from jax import lax
from jax.experimental import pallas as pl
from jax.experimental.pallas import tpu as pltpu
from jax.sharding import PartitionSpec as P

H = 128
L = 32
G = 6
FR = 16
NB = 14
EXT = NB + 2 * G
S = 8
T = 128
K = 64
PAIRS = 7
LAG = 2
MESH = pl.DeviceIdType.MESH
F32 = jnp.float32
BF = jnp.bfloat16


def dot(a, b):
    return jnp.dot(a, b, preferred_element_type=F32)


def split_np(values):
    import ml_dtypes

    high = values.astype(ml_dtypes.bfloat16)
    low = (values - high.astype(np.float64)).astype(ml_dtypes.bfloat16)
    return high, low


def transforms():
    k = np.arange(K)
    t = np.arange(T)
    angle = 2.0 * math.pi / T * ((k[:, None] * t[None, :]) % T)
    forward = np.concatenate([np.cos(angle), -np.sin(angle)], axis=0)
    fwd = np.concatenate(split_np(forward), axis=0)
    weight = (np.where(k == 0, 1.0, 2.0) / T)[None, :]
    inverse = np.concatenate([np.cos(angle.T) * weight, -np.sin(angle.T) * weight], axis=1)
    inv_hi, inv_lo = split_np(inverse)
    return jnp.asarray(fwd), jnp.asarray(inv_hi), jnp.asarray(inv_lo)


def rows(start, size):
    return pl.ds(pl.multiple_of(start, size), size)


def kernel(
    idx,
    pos3,
    edge_in,
    edge_out,
    edge_params,
    coord_w,
    node_in,
    node_out,
    node_bias,
    fwd,
    inv_hi,
    inv_lo,
    feats_hbm,
    spec_hbm,
    out,
    out_pos,
    ext,
    ghost,
    pt,
    po,
    near,
    scaled,
    acc_buf,
    send_buf,
    recv_buf,
    conv_buf,
    back_buf,
    spec,
    coef,
    mixed,
    node_buf,
    w_src,
    w_dst,
    w_edge,
    w_coord,
    w_n1,
    w_n2,
    loc_sem,
    pos_send,
    pos_recv,
    halo_send,
    halo_recv,
    msg_send,
    msg_recv,
    conv_send,
    conv_recv,
):
    sp = lax.axis_index("space")
    tm = lax.axis_index("tm")
    count = lax.axis_size("space")
    y = tm % 4
    half = tm // 4
    right = (sp + 1) % count
    left = (sp + count - 1) % count

    def partner_y(d):
        if d % 4 == 0:
            return y
        if d % 4 == 1:
            return y + 1 - 2 * (y % 2)
        if d % 4 == 2:
            return (y + 2) % 4
        return 3 - y

    def partner(d):
        return (1 - half if d >= 4 else half) * 4 + partner_y(d)

    barrier = pltpu.get_barrier_semaphore()
    for other in (left, right):
        pl.semaphore_signal(barrier, inc=1, device_id=(other, tm), device_id_type=MESH)
    for d in range(1, 8):
        pl.semaphore_signal(barrier, inc=1, device_id=(sp, partner(d)), device_id_type=MESH)

    own_copy = pltpu.make_async_copy(feats_hbm, ext.at[:, pl.ds(G, NB)], loc_sem.at[0])
    own_copy.start()
    spec_copy = pltpu.make_async_copy(spec_hbm, spec, loc_sem.at[1])
    spec_copy.start()

    group16 = lax.broadcasted_iota(jnp.int32, (FR, 128), 1) // L
    for b in range(NB):
        q, w = b // 4, b % 4
        tile = jnp.zeros((FR, 128), F32)
        for d in range(3):
            part = pos3[d, :, q * 128 : (q + 1) * 128]
            shift = (L * (d - w)) % 128
            if shift:
                part = pltpu.roll(part, shift, 1)
            tile = jnp.where(group16 == d, part, tile)
        pt[G + b] = tile

    pl.semaphore_wait(barrier, 9)

    def pos_copy(side):
        if side == 0:
            src, dst, dev = NB, 0, right
        else:
            src, dst, dev = G, G + NB, left
        return pltpu.make_async_remote_copy(
            src_ref=pt.at[pl.ds(src, G)],
            dst_ref=pt.at[pl.ds(dst, G)],
            send_sem=pos_send.at[side],
            recv_sem=pos_recv.at[side],
            device_id=(dev, tm),
            device_id_type=MESH,
        )

    def halo_copy(side, q):
        if side == 0:
            src, dev = NB - 1 - q, right
        else:
            src, dev = q, left
        return pltpu.make_async_remote_copy(
            src_ref=feats_hbm.at[:, src],
            dst_ref=ghost.at[side, q],
            send_sem=halo_send.at[side, q],
            recv_sem=halo_recv.at[side, q],
            device_id=(dev, tm),
            device_id_type=MESH,
        )

    def msg_copy(j, d):
        return pltpu.make_async_remote_copy(
            src_ref=send_buf.at[j, :, rows(partner_y(d) * 8, 8)],
            dst_ref=recv_buf.at[j, :, :, rows(tm * FR, FR), :],
            send_sem=msg_send.at[j, d - 1],
            recv_sem=msg_recv.at[j, d - 1],
            device_id=(sp, partner(d)),
            device_id_type=MESH,
        )

    def conv_copy(j, d):
        return pltpu.make_async_remote_copy(
            src_ref=conv_buf.at[j, :, :, rows(partner_y(d) * FR, FR), :],
            dst_ref=back_buf.at[j, :, y],
            send_sem=conv_send.at[j, d - 1],
            recv_sem=conv_recv.at[j, d - 1],
            device_id=(sp, partner(d)),
            device_id_type=MESH,
        )

    for side in range(2):
        pos_copy(side).start()
    for q in range(G):
        for side in range(2):
            halo_copy(side, q).start()

    def half_bf(v):
        return (v.astype(F32) * 0.5).astype(BF)

    zero = jnp.zeros((H, H), BF)
    src_half = half_bf(edge_in[:H, :])
    dst_half = half_bf(edge_in[H:, :])
    edge_half = half_bf(edge_out[...])
    row = lax.broadcasted_iota(jnp.int32, (H, H), 0)
    lane = lax.broadcasted_iota(jnp.int32, (H, H), 1)
    bias = edge_params[0:1, :] * 0.5
    dist_w = edge_params[1:2, :] * 0.5

    def split3(v):
        a = v.astype(BF).astype(F32)
        r = v - a
        b = r.astype(BF).astype(F32)
        return a, b, (r - b).astype(BF).astype(F32)

    bias_parts = split3(bias)
    dist_hi, dist_lo, _ = split3(dist_w)
    cw_hi = jnp.broadcast_to(coord_w[...], (H, H)).T
    cw_hi, cw_lo, _ = split3(cw_hi)
    for s in range(S):
        p, c = s // 2, (s % 2) * H
        w_src[p, :H, c : c + H] = src_half
        block = jnp.where((row == s) | (row == 8 + s), dist_hi, 0.0)
        block = jnp.where(row == 16 + s, dist_lo, block)
        for i in range(3):
            block = jnp.where(row == 24 + i, bias_parts[i], block)
        w_src[p, H:, c : c + H] = block.astype(BF)
        w_coord[p, c : c + H, :] = jnp.where(
            lane == s, cw_hi, jnp.where(lane == 8 + s, cw_lo, 0.0)
        ).astype(BF)
    for dst_ref, w in ((w_dst, dst_half), (w_edge, edge_half)):
        dst_ref[:H, :H] = w
        dst_ref[H:, H:] = w
        dst_ref[:H, H:] = zero
        dst_ref[H:, :H] = zero
    w_n1[...] = half_bf(node_in[:H, :])
    w_n2[...] = half_bf(node_in[H:, :])
    edge_bias = edge_params[2:3, :] * 0.5
    edge_bias2 = jnp.concatenate([edge_bias, edge_bias], axis=1)
    node_b0 = node_bias[0:1, :] * 0.5
    node_b1 = node_bias[1:2, :]

    for side in range(2):
        pos_copy(side).wait()
    own_copy.wait()

    group = lax.broadcasted_iota(jnp.int32, (8, 128), 1) // L

    def own_all(b):
        return jnp.concatenate([ext[f, G + b] for f in range(FR)], axis=0)

    def edge_block(j, e, b):
        augs = []
        for h in range(4):
            dist = jnp.zeros((8, 128), F32)
            for u in range(4):
                f = h * 4 + u
                base = (f * NB + b) * S
                for s in range(S):
                    near[f * 8 + s : f * 8 + s + 1, :] = pt[idx[base + s], f : f + 1, :]
                own = pt[G + b, f : f + 1, :]
                offset = own - near[f * 8 : (f + 1) * 8, :]
                square = offset * offset
                square = square + pltpu.roll(square, 64, 1)
                square = square + pltpu.roll(square, 32, 1)
                scaled[f * 8 : (f + 1) * 8, :] = offset / (1.0 + jnp.sqrt(square + 1.0))
                dist = jnp.where(group == u, square, dist)
            d_hi = dist.astype(BF).astype(F32)
            d_lo = (dist - d_hi).astype(BF).astype(F32)
            aug = jnp.concatenate(
                [d_hi, d_lo, d_hi, jnp.ones((8, 128), F32), jnp.zeros((96, 128), F32)], axis=0
            )
            augs.append(aug.T.astype(BF))
        first = jnp.concatenate([own_all(b), jnp.concatenate(augs, axis=0)], axis=1)
        acc = None
        wsum = None
        for p in range(4):
            cols = []
            for s in (2 * p, 2 * p + 1):
                cols.append(
                    jnp.concatenate(
                        [ext[f, idx[(f * NB + b) * S + s]] for f in range(FR)], axis=0
                    )
                )
            second = jnp.concatenate(cols, axis=1)
            pre = dot(first, w_src[p]) + dot(second, w_dst[...])
            hidden = (pre * jnp.tanh(pre) + pre).astype(BF)
            act = dot(hidden, w_edge[...]) + edge_bias2
            msg = act * jnp.tanh(act) + act
            both = msg[:, :H] + msg[:, H:]
            part = dot(msg.astype(BF), w_coord[p])
            acc = both if p == 0 else acc + both
            wsum = part if p == 0 else wsum + part
        acc_buf[...] = acc * (1.0 / S)
        for h in range(4):
            wt = wsum[h * 128 : (h + 1) * 128, :].T
            wv = wt[0:8, :] + wt[8:16, :]
            for u in range(4):
                f = h * 4 + u
                one = jnp.where(group == u, wv, 0.0)
                one = one + pltpu.roll(one, 64, 1)
                one = one + pltpu.roll(one, 32, 1)
                moved = jnp.sum(scaled[f * 8 : (f + 1) * 8, :] * one, axis=0, keepdims=True)
                own = pt[G + b, f : f + 1, :]
                po[pl.ds(b * FR + f, 1), :] = own + moved * (1.0 / S)
        for l in range(L):
            send_buf[j, e, l] = acc_buf[pl.ds(l, FR, stride=L), :].astype(BF)
        recv_buf[j, e, :, rows(tm * FR, FR), :] = send_buf[j, e, rows(y * 8, 8)]

    def edge_pair(j):
        @pl.when(j >= 1)
        def _():
            q = j - 1
            for side in range(2):
                halo_copy(side, q).wait_recv()
            for f in range(FR):
                ext[f, G - 1 - q] = ghost[0, q, f]
                ext[f, G + NB + q] = ghost[1, q, f]

        edge_block(j, 0, 6 - j)
        edge_block(j, 1, 7 + j)
        for d in (4, 5, 7, 6, 1, 3, 2):
            msg_copy(j, d).start()

    def spectral_pair(j):
        for d in range(1, 8):
            msg_copy(j, d).wait_recv()
        for e in range(2):

            def analyse(i, carry):
                r = 2 * i
                c2 = dot(
                    fwd[...],
                    jnp.concatenate([recv_buf[j, e, r], recv_buf[j, e, r + 1]], axis=1),
                )
                c = c2[:T] + c2[T:]
                coef[rows((e * 8 + r) * T, T), :] = c[:, :H]
                coef[rows((e * 8 + r + 1) * T, T), :] = c[:, H:]
                return carry

            lax.fori_loop(0, 4, analyse, 0, unroll=True)

        def mode(k, carry):
            re = coef[pl.ds(k, 16, stride=T), :].astype(BF)
            im = coef[pl.ds(K + k, 16, stride=T), :].astype(BF)
            lhs = jnp.concatenate(
                [jnp.concatenate([re, -im], axis=1), jnp.concatenate([im, re], axis=1)], axis=0
            )
            w = jnp.concatenate([spec[0, k], spec[1, k]], axis=0)
            m = dot(lhs, w)
            mixed[rows(k * 16, 16), :] = m[:16]
            mixed[rows((K + k) * 16, 16), :] = m[16:]
            return carry

        lax.fori_loop(0, K, mode, 0, unroll=8)
        rows_t = rows(half * 64, 64)
        inv = jnp.concatenate([inv_hi[rows_t, :], inv_lo[rows_t, :]], axis=0)
        for e in range(2):

            def synth(i, carry):
                r = 2 * i
                m = jnp.concatenate(
                    [mixed[pl.ds(e * 8 + r + n, T, stride=16), :] for n in range(2)], axis=1
                )
                hi = m.astype(BF)
                lo = (m - hi.astype(F32)).astype(BF)
                c2 = dot(inv, hi)
                c = (c2[:64] + c2[64:] + dot(inv[:64], lo)).astype(BF)
                conv_buf[j, e, r] = c[:, :H]
                conv_buf[j, e, r + 1] = c[:, H:]
                return carry

            lax.fori_loop(0, 4, synth, 0, unroll=True)
        for d in (1, 3, 2):
            conv_copy(j, d).start()
        for e in range(2):
            back_buf[j, e, y] = conv_buf[j, e, :, rows(y * FR, FR), :]

    def node_pair(j):
        for d in (1, 3, 2):
            conv_copy(j, d).wait_recv()
        for e in range(2):
            b = 6 - j if e == 0 else 7 + j
            node_buf[...] = dot(back_buf[j, e].reshape(L * FR, H), w_n2[...])
            part = jnp.concatenate(
                [node_buf[pl.ds(f, L, stride=FR), :] for f in range(FR)], axis=0
            )
            own = own_all(b)
            pre = dot(own, w_n1[...]) + part + node_b0
            hidden = (pre * jnp.tanh(pre) + pre).astype(BF)
            res = own.astype(F32) + (dot(hidden, node_out[...]) + node_b1)
            res = res.astype(BF)
            for f in range(FR):
                out[f, rows(b * L, L), :] = res[f * L : (f + 1) * L]

    def step(j, carry):
        @pl.when(j < PAIRS)
        def _():
            edge_pair(j)

        @pl.when(j > LAG)
        def _():
            node_pair(j - LAG - 1)

        @pl.when(j == LAG)
        def _():
            spec_copy.wait()

        @pl.when((j >= LAG) & (j < PAIRS + LAG))
        def _():
            spectral_pair(j - LAG)

        return carry

    lax.fori_loop(0, PAIRS + LAG + 1, step, 0)

    for d in range(3):
        for q in range(4):
            tile = jnp.zeros((FR, 128), F32)
            for w in range(4):
                b = q * 4 + w
                if b < NB:
                    part = po[b * FR : (b + 1) * FR, :]
                    shift = (L * (w - d)) % 128
                    if shift:
                        part = pltpu.roll(part, shift, 1)
                    tile = jnp.where(group16 == w, part, tile)
            out_pos[d, :, q * 128 : (q + 1) * 128] = tile

    for side in range(2):
        for q in range(G):
            halo_copy(side, q).wait_send()

    def drain(j, carry):
        for d in range(1, 8):
            msg_copy(j, d).wait_send()
        for d in range(1, 4):
            conv_copy(j, d).wait_send()
        return carry

    lax.fori_loop(0, PAIRS, drain, 0)


def shards(
    node_feats,
    positions,
    neighbours,
    edge_in,
    edge_out,
    edge_params,
    coord_weight,
    spectral,
    node_in,
    node_out,
    node_bias,
):
    first = lax.axis_index("space") * NB - G
    total = NB * lax.axis_size("space")
    idx = ((neighbours - first) % total).reshape(-1)
    pos3 = jnp.pad(jnp.transpose(positions, (1, 0, 2)), ((0, 0), (0, 0), (0, 64)))
    fwd, inv_hi, inv_lo = transforms()
    vmem = pl.BlockSpec(memory_space=pltpu.VMEM)
    hbm = pl.BlockSpec(memory_space=pl.ANY)
    dma = pltpu.SemaphoreType.DMA
    new_feats, pos_out = pl.pallas_call(
        kernel,
        out_shape=(
            jax.ShapeDtypeStruct((FR, NB * L, H), BF),
            jax.ShapeDtypeStruct((3, FR, 512), F32),
        ),
        in_specs=[pl.BlockSpec(memory_space=pltpu.SMEM)] + [vmem] * 11 + [hbm] * 2,
        out_specs=(vmem, vmem),
        scratch_shapes=[
            pltpu.VMEM((FR, EXT, L, H), BF),
            pltpu.VMEM((2, G, FR, L, H), BF),
            pltpu.VMEM((EXT, FR, 128), F32),
            pltpu.VMEM((NB * FR, 128), F32),
            pltpu.VMEM((FR * S, 128), F32),
            pltpu.VMEM((FR * S, 128), F32),
            pltpu.VMEM((FR * L, H), F32),
            pltpu.VMEM((PAIRS, 2, L, FR, H), BF),
            pltpu.VMEM((PAIRS, 2, 8, T, H), BF),
            pltpu.VMEM((PAIRS, 2, 8, 64, H), BF),
            pltpu.VMEM((PAIRS, 2, 4, 8, FR, H), BF),
            pltpu.VMEM((2, K, H, H), BF),
            pltpu.VMEM((16 * T, H), F32),
            pltpu.VMEM((16 * T, H), F32),
            pltpu.VMEM((FR * L, H), F32),
            pltpu.VMEM((4, 2 * H, 2 * H), BF),
            pltpu.VMEM((2 * H, 2 * H), BF),
            pltpu.VMEM((2 * H, 2 * H), BF),
            pltpu.VMEM((4, 2 * H, H), BF),
            pltpu.VMEM((H, H), BF),
            pltpu.VMEM((H, H), BF),
            dma((2,)),
            dma((2,)),
            dma((2,)),
            dma((2, G)),
            dma((2, G)),
            dma((PAIRS, 7)),
            dma((PAIRS, 7)),
            dma((PAIRS, 3)),
            dma((PAIRS, 3)),
        ],
        compiler_params=pltpu.CompilerParams(
            collective_id=0, has_side_effects=True, vmem_limit_bytes=56 * 1024 * 1024
        ),
    )(
        idx,
        pos3,
        edge_in,
        edge_out,
        edge_params,
        coord_weight.reshape(1, H),
        node_in,
        node_out,
        node_bias,
        fwd,
        inv_hi,
        inv_lo,
        node_feats.reshape(FR, NB, L, H),
        spectral,
    )
    new_positions = jnp.transpose(pos_out, (1, 0, 2))[:, :, : NB * L]
    return (new_feats, new_positions)


def solution(mesh):
    placed = (
        P("tm", "space", None),
        P("tm", None, "space"),
        P("tm", "space", None),
        P(),
        P(),
        P(),
        P(),
        P(),
        P(),
        P(),
        P(),
    )
    return jax.shard_map(
        shards,
        mesh=mesh,
        in_specs=placed,
        out_specs=(P("tm", "space", None), P("tm", None, "space")),
        check_vma=False,
    )
```

```python
import math

import jax
import jax.numpy as jnp
import numpy as np
from jax import lax
from jax.experimental import pallas as pl
from jax.experimental.pallas import tpu as pltpu
from jax.sharding import PartitionSpec as P

H = 128
L = 32
G = 6
FR = 16
NB = 14
EXT = NB + 2 * G
S = 8
T = 128
K = 64
PAIRS = 7
LAG = 1
MESH = pl.DeviceIdType.MESH
F32 = jnp.float32
BF = jnp.bfloat16


def dot(a, b):
    return jnp.dot(a, b, preferred_element_type=F32)


def split_np(values):
    import ml_dtypes

    high = values.astype(ml_dtypes.bfloat16)
    low = (values - high.astype(np.float64)).astype(ml_dtypes.bfloat16)
    return high, low


def transforms():
    k = np.arange(K)
    t = np.arange(T)
    angle = 2.0 * math.pi / T * ((k[:, None] * t[None, :]) % T)
    forward = np.concatenate([np.cos(angle), -np.sin(angle)], axis=0)
    fwd = np.concatenate(split_np(forward), axis=0)
    weight = (np.where(k == 0, 1.0, 2.0) / T)[None, :]
    inverse = np.concatenate([np.cos(angle.T) * weight, -np.sin(angle.T) * weight], axis=1)
    inv_hi, inv_lo = split_np(inverse)
    return jnp.asarray(fwd), jnp.asarray(inv_hi), jnp.asarray(inv_lo)


def rows(start, size):
    return pl.ds(pl.multiple_of(start, size), size)


def kernel(
    idx,
    pos3,
    edge_in,
    edge_out,
    edge_params,
    coord_w,
    node_in,
    node_out,
    node_bias,
    fwd,
    inv_hi,
    inv_lo,
    feats_hbm,
    spec_hbm,
    out,
    out_pos,
    ext,
    ghost,
    pos_ghost,
    pt,
    po,
    near,
    scaled,
    acc_buf,
    send_buf,
    recv_buf,
    conv_buf,
    back_buf,
    spec,
    coef,
    mixed,
    node_buf,
    w_src,
    w_dst,
    w_edge,
    w_coord,
    w_n1,
    w_n2,
    loc_sem,
    pos_send,
    pos_recv,
    halo_send,
    halo_recv,
    msg_send,
    msg_recv,
    conv_send,
    conv_recv,
):
    sp = lax.axis_index("space")
    tm = lax.axis_index("tm")
    count = lax.axis_size("space")
    y = tm % 4
    half = tm // 4
    total = NB * count
    first_block = sp * NB - G
    right = (sp + 1) % count
    left = (sp + count - 1) % count

    def partner_y(d):
        if d % 4 == 0:
            return y
        if d % 4 == 1:
            return y + 1 - 2 * (y % 2)
        if d % 4 == 2:
            return (y + 2) % 4
        return 3 - y

    def partner(d):
        return (1 - half if d >= 4 else half) * 4 + partner_y(d)

    barrier = pltpu.get_barrier_semaphore()
    for other in (left, right):
        pl.semaphore_signal(barrier, inc=1, device_id=(other, tm), device_id_type=MESH)
    for d in range(1, 8):
        pl.semaphore_signal(barrier, inc=1, device_id=(sp, partner(d)), device_id_type=MESH)

    own_copy = pltpu.make_async_copy(feats_hbm, ext.at[:, pl.ds(G, NB)], loc_sem.at[0])
    own_copy.start()
    spec_copy = pltpu.make_async_copy(spec_hbm, spec, loc_sem.at[1])
    spec_copy.start()

    pl.semaphore_wait(barrier, 9)

    def pos_copy(side):
        if side == 0:
            src, dev = NB, right
        else:
            src, dev = G, left
        return pltpu.make_async_remote_copy(
            src_ref=pt.at[pl.ds(src, G)],
            dst_ref=pos_ghost.at[side],
            send_sem=pos_send.at[side],
            recv_sem=pos_recv.at[side],
            device_id=(dev, tm),
            device_id_type=MESH,
        )

    def halo_copy(side, q):
        if side == 0:
            src, dev = NB - 1 - q, right
        else:
            src, dev = q, left
        return pltpu.make_async_remote_copy(
            src_ref=feats_hbm.at[:, src],
            dst_ref=ghost.at[side, q],
            send_sem=halo_send.at[side, q],
            recv_sem=halo_recv.at[side, q],
            device_id=(dev, tm),
            device_id_type=MESH,
        )

    def msg_copy(j, d):
        return pltpu.make_async_remote_copy(
            src_ref=send_buf.at[j, :, rows(partner_y(d) * 8, 8)],
            dst_ref=recv_buf.at[j, :, :, rows(tm * FR, FR), :],
            send_sem=msg_send.at[j, d - 1],
            recv_sem=msg_recv.at[j, d - 1],
            device_id=(sp, partner(d)),
            device_id_type=MESH,
        )

    def conv_copy(j, d):
        return pltpu.make_async_remote_copy(
            src_ref=conv_buf.at[j, :, :, rows(partner_y(d) * FR, FR), :],
            dst_ref=back_buf.at[j, :, y],
            send_sem=conv_send.at[j, d - 1],
            recv_sem=conv_recv.at[j, d - 1],
            device_id=(sp, partner(d)),
            device_id_type=MESH,
        )

    for q in range(G):
        for side in range(2):
            halo_copy(side, q).start()

    group16 = lax.broadcasted_iota(jnp.int32, (FR, 128), 1) // L
    for b in range(NB):
        q, w = b // 4, b % 4
        tile = jnp.zeros((FR, 128), F32)
        for d in range(3):
            if q < 3:
                part = pos3[d, :, q * 128 : (q + 1) * 128]
            else:
                part = jnp.concatenate(
                    [pos3[d, :, 384:448], jnp.zeros((FR, 64), F32)], axis=1
                )
            shift = (L * (d - w)) % 128
            if shift:
                part = pltpu.roll(part, shift, 1)
            tile = jnp.where(group16 == d, part, tile)
        pt[G + b] = tile

    for side in range(2):
        pos_copy(side).start()

    def half_bf(v):
        return (v.astype(F32) * 0.5).astype(BF)

    zero = jnp.zeros((H, H), BF)
    src_half = half_bf(edge_in[:H, :])
    dst_half = half_bf(edge_in[H:, :])
    edge_half = half_bf(edge_out[...])
    row = lax.broadcasted_iota(jnp.int32, (H, H), 0)
    lane = lax.broadcasted_iota(jnp.int32, (H, H), 1)
    bias = edge_params[0:1, :] * 0.5
    dist_w = edge_params[1:2, :] * 0.5

    def split3(v):
        a = v.astype(BF).astype(F32)
        r = v - a
        b = r.astype(BF).astype(F32)
        return a, b, (r - b).astype(BF).astype(F32)

    bias_parts = split3(bias)
    dist_hi, dist_lo, _ = split3(dist_w)
    cw_hi = jnp.broadcast_to(coord_w[...], (H, H)).T
    cw_hi, cw_lo, _ = split3(cw_hi)
    for s in range(S):
        p, c = s // 2, (s % 2) * H
        w_src[p, :H, c : c + H] = src_half
        block = jnp.where((row == s) | (row == 8 + s), dist_hi, 0.0)
        block = jnp.where(row == 16 + s, dist_lo, block)
        for i in range(3):
            block = jnp.where(row == 24 + i, bias_parts[i], block)
        w_src[p, H:, c : c + H] = block.astype(BF)
        w_coord[p, c : c + H, :] = jnp.where(
            lane == s, cw_hi, jnp.where(lane == 8 + s, cw_lo, 0.0)
        ).astype(BF)
    for dst_ref, w in ((w_dst, dst_half), (w_edge, edge_half)):
        dst_ref[:H, :H] = w
        dst_ref[H:, H:] = w
        dst_ref[:H, H:] = zero
        dst_ref[H:, :H] = zero
    w_n1[...] = half_bf(node_in[:H, :])
    w_n2[...] = half_bf(node_in[H:, :])
    edge_bias = edge_params[2:3, :] * 0.5
    edge_bias2 = jnp.concatenate([edge_bias, edge_bias], axis=1)
    node_b0 = node_bias[0:1, :] * 0.5
    node_b1 = node_bias[1:2, :]

    own_copy.wait()

    group = lax.broadcasted_iota(jnp.int32, (8, 128), 1) // L

    def own_all(b):
        return jnp.concatenate([ext[f, G + b] for f in range(FR)], axis=0)

    def edge_block(j, e, b):
        picked = {}
        for f in range(FR):
            for s in range(S):
                v = idx[b, s, f] - first_block
                v = jnp.where(v < 0, v + total, v)
                v = jnp.where(v >= total, v - total, v)
                picked[f, s] = jnp.minimum(v, EXT - 1)
        augs = []
        for h in range(4):
            dist = jnp.zeros((8, 128), F32)
            for u in range(4):
                f = h * 4 + u
                for s in range(S):
                    near[f * 8 + s : f * 8 + s + 1, :] = pt[picked[f, s], f : f + 1, :]
                own = pt[G + b, f : f + 1, :]
                offset = own - near[f * 8 : (f + 1) * 8, :]
                square = offset * offset
                square = square + pltpu.roll(square, 64, 1)
                square = square + pltpu.roll(square, 32, 1)
                scaled[f * 8 : (f + 1) * 8, :] = offset / (1.0 + jnp.sqrt(square + 1.0))
                dist = jnp.where(group == u, square, dist)
            d_hi = dist.astype(BF).astype(F32)
            d_lo = (dist - d_hi).astype(BF).astype(F32)
            aug = jnp.concatenate(
                [d_hi, d_lo, d_hi, jnp.ones((8, 128), F32), jnp.zeros((96, 128), F32)], axis=0
            )
            augs.append(aug.T.astype(BF))
        first = jnp.concatenate([own_all(b), jnp.concatenate(augs, axis=0)], axis=1)
        acc = None
        wsum = None
        for p in range(4):
            cols = []
            for s in (2 * p, 2 * p + 1):
                cols.append(
                    jnp.concatenate(
                        [ext[f, picked[f, s]] for f in range(FR)], axis=0
                    )
                )
            second = jnp.concatenate(cols, axis=1)
            pre = dot(first, w_src[p]) + dot(second, w_dst[...])
            hidden = (pre * jnp.tanh(pre) + pre).astype(BF)
            act = dot(hidden, w_edge[...]) + edge_bias2
            msg = act * jnp.tanh(act) + act
            both = msg[:, :H] + msg[:, H:]
            part = dot(msg.astype(BF), w_coord[p])
            acc = both if p == 0 else acc + both
            wsum = part if p == 0 else wsum + part
        acc_buf[...] = acc * (1.0 / S)
        for h in range(4):
            wt = wsum[h * 128 : (h + 1) * 128, :].T
            wv = wt[0:8, :] + wt[8:16, :]
            for u in range(4):
                f = h * 4 + u
                one = jnp.where(group == u, wv, 0.0)
                one = one + pltpu.roll(one, 64, 1)
                one = one + pltpu.roll(one, 32, 1)
                moved = jnp.sum(scaled[f * 8 : (f + 1) * 8, :] * one, axis=0, keepdims=True)
                own = pt[G + b, f : f + 1, :]
                po[pl.ds(b * FR + f, 1), :] = own + moved * (1.0 / S)
        for l in range(L):
            send_buf[j, e, l] = acc_buf[pl.ds(l, FR, stride=L), :].astype(BF)
        recv_buf[j, e, :, rows(tm * FR, FR), :] = send_buf[j, e, rows(y * 8, 8)]

    def edge_pair(j):
        @pl.when(j == 1)
        def _():
            for side in range(2):
                pos_copy(side).wait()
            pt[:G] = pos_ghost[0]
            pt[G + NB :] = pos_ghost[1]

        @pl.when(j >= 1)
        def _():
            q = j - 1
            for side in range(2):
                halo_copy(side, q).wait_recv()
            for f in range(FR):
                ext[f, G - 1 - q] = ghost[0, q, f]
                ext[f, G + NB + q] = ghost[1, q, f]

        edge_block(j, 0, 6 - j)
        edge_block(j, 1, 7 + j)
        for d in (4, 5, 7, 6, 1, 3, 2):
            msg_copy(j, d).start()

    def spectral_pair(j):
        for d in range(1, 8):
            msg_copy(j, d).wait_recv()
        for e in range(2):

            def analyse(i, carry):
                r = 2 * i
                c2 = dot(
                    fwd[...],
                    jnp.concatenate([recv_buf[j, e, r], recv_buf[j, e, r + 1]], axis=1),
                )
                c = c2[:T] + c2[T:]
                coef[rows((e * 8 + r) * T, T), :] = c[:, :H]
                coef[rows((e * 8 + r + 1) * T, T), :] = c[:, H:]
                return carry

            lax.fori_loop(0, 4, analyse, 0, unroll=True)

        def mode(k, carry):
            re = coef[pl.ds(k, 16, stride=T), :].astype(BF)
            im = coef[pl.ds(K + k, 16, stride=T), :].astype(BF)
            lhs = jnp.concatenate(
                [jnp.concatenate([re, -im], axis=1), jnp.concatenate([im, re], axis=1)], axis=0
            )
            w = jnp.concatenate([spec[0, k], spec[1, k]], axis=0)
            m = dot(lhs, w)
            mixed[rows(k * 16, 16), :] = m[:16]
            mixed[rows((K + k) * 16, 16), :] = m[16:]
            return carry

        lax.fori_loop(0, K, mode, 0, unroll=8)
        rows_t = rows(half * 64, 64)
        inv = jnp.concatenate([inv_hi[rows_t, :], inv_lo[rows_t, :]], axis=0)
        for e in range(2):

            def synth(i, carry):
                r = 2 * i
                m = jnp.concatenate(
                    [mixed[pl.ds(e * 8 + r + n, T, stride=16), :] for n in range(2)], axis=1
                )
                hi = m.astype(BF)
                lo = (m - hi.astype(F32)).astype(BF)
                c2 = dot(inv, hi)
                c = (c2[:64] + c2[64:] + dot(inv[:64], lo)).astype(BF)
                conv_buf[j, e, r] = c[:, :H]
                conv_buf[j, e, r + 1] = c[:, H:]
                return carry

            lax.fori_loop(0, 4, synth, 0, unroll=True)
        for d in (1, 3, 2):
            conv_copy(j, d).start()
        for e in range(2):
            back_buf[j, e, y] = conv_buf[j, e, :, rows(y * FR, FR), :]

    def node_pair(j):
        for d in (1, 3, 2):
            conv_copy(j, d).wait_recv()
        for e in range(2):
            b = 6 - j if e == 0 else 7 + j
            node_buf[...] = dot(back_buf[j, e].reshape(L * FR, H), w_n2[...])
            part = jnp.concatenate(
                [node_buf[pl.ds(f, L, stride=FR), :] for f in range(FR)], axis=0
            )
            own = own_all(b)
            pre = dot(own, w_n1[...]) + part + node_b0
            hidden = (pre * jnp.tanh(pre) + pre).astype(BF)
            res = own.astype(F32) + (dot(hidden, node_out[...]) + node_b1)
            res = res.astype(BF)
            for f in range(FR):
                out[f, rows(b * L, L), :] = res[f * L : (f + 1) * L]

    def step(j, carry):
        @pl.when(j < PAIRS)
        def _():
            edge_pair(j)

        @pl.when(j > LAG)
        def _():
            node_pair(j - LAG - 1)

        @pl.when(j == LAG)
        def _():
            spec_copy.wait()

        @pl.when((j >= LAG) & (j < PAIRS + LAG))
        def _():
            spectral_pair(j - LAG)

        return carry

    lax.fori_loop(0, PAIRS + LAG + 1, step, 0)

    for d in range(3):
        for q in range(4):
            tile = jnp.zeros((FR, 128), F32)
            for w in range(4):
                b = q * 4 + w
                if b < NB:
                    part = po[b * FR : (b + 1) * FR, :]
                    shift = (L * (w - d)) % 128
                    if shift:
                        part = pltpu.roll(part, shift, 1)
                    tile = jnp.where(group16 == w, part, tile)
            width = min(128, NB * L - q * 128)
            out_pos[d, :, q * 128 : q * 128 + width] = tile[:, :width]

    for side in range(2):
        for q in range(G):
            halo_copy(side, q).wait_send()

    def drain(j, carry):
        for d in range(1, 8):
            msg_copy(j, d).wait_send()
        for d in range(1, 4):
            conv_copy(j, d).wait_send()
        return carry

    lax.fori_loop(0, PAIRS, drain, 0)


def shards(
    node_feats,
    positions,
    neighbours,
    edge_in,
    edge_out,
    edge_params,
    coord_weight,
    spectral,
    node_in,
    node_out,
    node_bias,
):
    idx = jnp.transpose(neighbours, (1, 2, 0))
    pos3 = jnp.transpose(positions, (1, 0, 2))
    fwd, inv_hi, inv_lo = transforms()
    vmem = pl.BlockSpec(memory_space=pltpu.VMEM)
    hbm = pl.BlockSpec(memory_space=pl.ANY)
    dma = pltpu.SemaphoreType.DMA
    new_feats, pos_out = pl.pallas_call(
        kernel,
        out_shape=(
            pltpu.VMEM((FR, NB * L, H), BF),
            pltpu.VMEM((3, FR, NB * L), F32),
        ),
        in_specs=[pl.BlockSpec(memory_space=pltpu.SMEM)] + [vmem] * 11 + [hbm] * 2,
        out_specs=(vmem, vmem),
        scratch_shapes=[
            pltpu.VMEM((FR, EXT, L, H), BF),
            pltpu.VMEM((2, G, FR, L, H), BF),
            pltpu.VMEM((2, G, FR, 128), F32),
            pltpu.VMEM((EXT, FR, 128), F32),
            pltpu.VMEM((NB * FR, 128), F32),
            pltpu.VMEM((FR * S, 128), F32),
            pltpu.VMEM((FR * S, 128), F32),
            pltpu.VMEM((FR * L, H), F32),
            pltpu.VMEM((PAIRS, 2, L, FR, H), BF),
            pltpu.VMEM((PAIRS, 2, 8, T, H), BF),
            pltpu.VMEM((PAIRS, 2, 8, 64, H), BF),
            pltpu.VMEM((PAIRS, 2, 4, 8, FR, H), BF),
            pltpu.VMEM((2, K, H, H), BF),
            pltpu.VMEM((16 * T, H), F32),
            pltpu.VMEM((16 * T, H), F32),
            pltpu.VMEM((FR * L, H), F32),
            pltpu.VMEM((4, 2 * H, 2 * H), BF),
            pltpu.VMEM((2 * H, 2 * H), BF),
            pltpu.VMEM((2 * H, 2 * H), BF),
            pltpu.VMEM((4, 2 * H, H), BF),
            pltpu.VMEM((H, H), BF),
            pltpu.VMEM((H, H), BF),
            dma((2,)),
            dma((2,)),
            dma((2,)),
            dma((2, G)),
            dma((2, G)),
            dma((PAIRS, 7)),
            dma((PAIRS, 7)),
            dma((PAIRS, 3)),
            dma((PAIRS, 3)),
        ],
        compiler_params=pltpu.CompilerParams(
            collective_id=0, has_side_effects=True, vmem_limit_bytes=56 * 1024 * 1024
        ),
    )(
        idx,
        pos3,
        edge_in,
        edge_out,
        edge_params,
        coord_weight.reshape(1, H),
        node_in,
        node_out,
        node_bias,
        fwd,
        inv_hi,
        inv_lo,
        node_feats.reshape(FR, NB, L, H),
        spectral,
    )
    new_positions = jnp.transpose(pos_out, (1, 0, 2))
    return (new_feats, new_positions)


def solution(mesh):
    placed = (
        P("tm", "space", None),
        P("tm", None, "space"),
        P("tm", "space", None),
        P(),
        P(),
        P(),
        P(),
        P(),
        P(),
        P(),
        P(),
    )
    return jax.shard_map(
        shards,
        mesh=mesh,
        in_specs=placed,
        out_specs=(P("tm", "space", None), P("tm", None, "space")),
        check_vma=False,
    )
```

```python
import math

import jax
import jax.numpy as jnp
import numpy as np
from jax import lax
from jax.experimental import pallas as pl
from jax.experimental.pallas import tpu as pltpu
from jax.sharding import PartitionSpec as P

H = 128
L = 32
G = 6
FR = 16
NB = 14
EXT = NB + 2 * G
S = 8
T = 128
K = 64
PAIRS = 7
LAG = 1
MESH = pl.DeviceIdType.MESH
F32 = jnp.float32
BF = jnp.bfloat16


def dot(a, b):
    return jnp.dot(a, b, preferred_element_type=F32)


def split_np(values):
    import ml_dtypes

    high = values.astype(ml_dtypes.bfloat16)
    low = (values - high.astype(np.float64)).astype(ml_dtypes.bfloat16)
    return high, low


def transforms():
    k = np.arange(K)
    t = np.arange(T)
    angle = 2.0 * math.pi / T * ((k[:, None] * t[None, :]) % T)
    forward = np.concatenate([np.cos(angle), -np.sin(angle)], axis=0)
    fwd = np.concatenate(split_np(forward), axis=0)
    weight = (np.where(k == 0, 1.0, 2.0) / T)[None, :]
    inverse = np.concatenate([np.cos(angle.T) * weight, -np.sin(angle.T) * weight], axis=1)
    inv_hi, inv_lo = split_np(inverse)
    return jnp.asarray(fwd), jnp.asarray(inv_hi), jnp.asarray(inv_lo)


def rows(start, size):
    return pl.ds(pl.multiple_of(start, size), size)


def kernel(
    idx,
    pos3,
    edge_in,
    edge_out,
    edge_params,
    coord_w,
    node_in,
    node_out,
    node_bias,
    fwd,
    inv_hi,
    inv_lo,
    feats_hbm,
    spec_hbm,
    out,
    out_pos,
    ext,
    ghost,
    pos_ghost,
    pt,
    po,
    near,
    scaled,
    acc_buf,
    send_buf,
    recv_buf,
    conv_buf,
    back_buf,
    spec,
    coef,
    mixed,
    node_buf,
    w_src,
    w_dst,
    w_edge,
    w_coord,
    w_n1,
    w_n2,
    loc_sem,
    pos_send,
    pos_recv,
    halo_send,
    halo_recv,
    msg_send,
    msg_recv,
    conv_send,
    conv_recv,
):
    sp = lax.axis_index("space")
    tm = lax.axis_index("tm")
    count = lax.axis_size("space")
    y = tm % 4
    half = tm // 4
    total = NB * count
    first_block = sp * NB - G
    right = (sp + 1) % count
    left = (sp + count - 1) % count

    def partner_y(d):
        if d % 4 == 0:
            return y
        if d % 4 == 1:
            return y + 1 - 2 * (y % 2)
        if d % 4 == 2:
            return (y + 2) % 4
        return 3 - y

    def partner(d):
        return (1 - half if d >= 4 else half) * 4 + partner_y(d)

    barrier = pltpu.get_barrier_semaphore()
    for other in (left, right):
        pl.semaphore_signal(barrier, inc=1, device_id=(other, tm), device_id_type=MESH)
    for d in range(1, 8):
        pl.semaphore_signal(barrier, inc=1, device_id=(sp, partner(d)), device_id_type=MESH)

    own_copy = pltpu.make_async_copy(feats_hbm, ext.at[:, pl.ds(G, NB)], loc_sem.at[0])
    own_copy.start()
    spec_copy = pltpu.make_async_copy(spec_hbm, spec, loc_sem.at[1])
    spec_copy.start()

    pl.semaphore_wait(barrier, 9)

    def pos_copy(side):
        if side == 0:
            src, dev = NB, right
        else:
            src, dev = G, left
        return pltpu.make_async_remote_copy(
            src_ref=pt.at[pl.ds(src, G)],
            dst_ref=pos_ghost.at[side],
            send_sem=pos_send.at[side],
            recv_sem=pos_recv.at[side],
            device_id=(dev, tm),
            device_id_type=MESH,
        )

    def halo_copy(side, q):
        if side == 0:
            src, dev = NB - 1 - q, right
        else:
            src, dev = q, left
        return pltpu.make_async_remote_copy(
            src_ref=feats_hbm.at[:, src],
            dst_ref=ghost.at[side, q],
            send_sem=halo_send.at[side, q],
            recv_sem=halo_recv.at[side, q],
            device_id=(dev, tm),
            device_id_type=MESH,
        )

    def msg_copy(j, e, d):
        return pltpu.make_async_remote_copy(
            src_ref=send_buf.at[j, e, rows(partner_y(d) * 8, 8)],
            dst_ref=recv_buf.at[j, e, :, rows(tm * FR, FR), :],
            send_sem=msg_send.at[j, e, d - 1],
            recv_sem=msg_recv.at[j, e, d - 1],
            device_id=(sp, partner(d)),
            device_id_type=MESH,
        )

    def conv_copy(j, e, d):
        return pltpu.make_async_remote_copy(
            src_ref=conv_buf.at[j, e, :, rows(partner_y(d) * FR, FR), :],
            dst_ref=back_buf.at[j, e, y],
            send_sem=conv_send.at[j, e, d - 1],
            recv_sem=conv_recv.at[j, e, d - 1],
            device_id=(sp, partner(d)),
            device_id_type=MESH,
        )

    for q in range(G):
        for side in range(2):
            halo_copy(side, q).start()

    group16 = lax.broadcasted_iota(jnp.int32, (FR, 128), 1) // L
    for b in range(NB):
        q, w = b // 4, b % 4
        tile = jnp.zeros((FR, 128), F32)
        for d in range(3):
            if q < 3:
                part = pos3[d, :, q * 128 : (q + 1) * 128]
            else:
                part = jnp.concatenate(
                    [pos3[d, :, 384:448], jnp.zeros((FR, 64), F32)], axis=1
                )
            shift = (L * (d - w)) % 128
            if shift:
                part = pltpu.roll(part, shift, 1)
            tile = jnp.where(group16 == d, part, tile)
        pt[G + b] = tile

    for side in range(2):
        pos_copy(side).start()

    def half_bf(v):
        return (v.astype(F32) * 0.5).astype(BF)

    zero = jnp.zeros((H, H), BF)
    src_half = half_bf(edge_in[:H, :])
    dst_half = half_bf(edge_in[H:, :])
    edge_half = half_bf(edge_out[...])
    row = lax.broadcasted_iota(jnp.int32, (H, H), 0)
    lane = lax.broadcasted_iota(jnp.int32, (H, H), 1)
    bias = edge_params[0:1, :] * 0.5
    dist_w = edge_params[1:2, :] * 0.5

    def split3(v):
        a = v.astype(BF).astype(F32)
        r = v - a
        b = r.astype(BF).astype(F32)
        return a, b, (r - b).astype(BF).astype(F32)

    bias_parts = split3(bias)
    dist_hi, dist_lo, _ = split3(dist_w)
    cw_hi = jnp.broadcast_to(coord_w[...], (H, H)).T
    cw_hi, cw_lo, _ = split3(cw_hi)
    for s in range(S):
        p, c = s // 2, (s % 2) * H
        w_src[p, :H, c : c + H] = src_half
        block = jnp.where((row == s) | (row == 8 + s), dist_hi, 0.0)
        block = jnp.where(row == 16 + s, dist_lo, block)
        for i in range(3):
            block = jnp.where(row == 24 + i, bias_parts[i], block)
        w_src[p, H:, c : c + H] = block.astype(BF)
        w_coord[p, c : c + H, :] = jnp.where(
            lane == s, cw_hi, jnp.where(lane == 8 + s, cw_lo, 0.0)
        ).astype(BF)
    for dst_ref, w in ((w_dst, dst_half), (w_edge, edge_half)):
        dst_ref[:H, :H] = w
        dst_ref[H:, H:] = w
        dst_ref[:H, H:] = zero
        dst_ref[H:, :H] = zero
    w_n1[...] = half_bf(node_in[:H, :])
    w_n2[...] = half_bf(node_in[H:, :])
    edge_bias = edge_params[2:3, :] * 0.5
    edge_bias2 = jnp.concatenate([edge_bias, edge_bias], axis=1)
    node_b0 = node_bias[0:1, :] * 0.5
    node_b1 = node_bias[1:2, :]

    own_copy.wait()

    group = lax.broadcasted_iota(jnp.int32, (8, 128), 1) // L

    def own_all(b):
        return jnp.concatenate([ext[f, G + b] for f in range(FR)], axis=0)

    def edge_block(j, e, b):
        picked = {}
        for f in range(FR):
            for s in range(S):
                v = idx[b, s, f] - first_block
                v = jnp.where(v < 0, v + total, v)
                v = jnp.where(v >= total, v - total, v)
                picked[f, s] = jnp.minimum(v, EXT - 1)
        augs = []
        for h in range(4):
            dist = jnp.zeros((8, 128), F32)
            for u in range(4):
                f = h * 4 + u
                for s in range(S):
                    near[f * 8 + s : f * 8 + s + 1, :] = pt[picked[f, s], f : f + 1, :]
                own = pt[G + b, f : f + 1, :]
                offset = own - near[f * 8 : (f + 1) * 8, :]
                square = offset * offset
                square = square + pltpu.roll(square, 64, 1)
                square = square + pltpu.roll(square, 32, 1)
                scaled[f * 8 : (f + 1) * 8, :] = offset / (1.0 + jnp.sqrt(square + 1.0))
                dist = jnp.where(group == u, square, dist)
            d_hi = dist.astype(BF).astype(F32)
            d_lo = (dist - d_hi).astype(BF).astype(F32)
            aug = jnp.concatenate(
                [d_hi, d_lo, d_hi, jnp.ones((8, 128), F32), jnp.zeros((96, 128), F32)], axis=0
            )
            augs.append(aug.T.astype(BF))
        first = jnp.concatenate([own_all(b), jnp.concatenate(augs, axis=0)], axis=1)
        acc = None
        wsum = None
        for p in range(4):
            cols = []
            for s in (2 * p, 2 * p + 1):
                cols.append(
                    jnp.concatenate(
                        [ext[f, picked[f, s]] for f in range(FR)], axis=0
                    )
                )
            second = jnp.concatenate(cols, axis=1)
            pre = dot(first, w_src[p]) + dot(second, w_dst[...])
            hidden = (pre * jnp.tanh(pre) + pre).astype(BF)
            act = dot(hidden, w_edge[...]) + edge_bias2
            msg = act * jnp.tanh(act) + act
            both = msg[:, :H] + msg[:, H:]
            part = dot(msg.astype(BF), w_coord[p])
            acc = both if p == 0 else acc + both
            wsum = part if p == 0 else wsum + part
        acc_buf[...] = acc * (1.0 / S)
        for h in range(4):
            wt = wsum[h * 128 : (h + 1) * 128, :].T
            wv = wt[0:8, :] + wt[8:16, :]
            for u in range(4):
                f = h * 4 + u
                one = jnp.where(group == u, wv, 0.0)
                one = one + pltpu.roll(one, 64, 1)
                one = one + pltpu.roll(one, 32, 1)
                moved = jnp.sum(scaled[f * 8 : (f + 1) * 8, :] * one, axis=0, keepdims=True)
                own = pt[G + b, f : f + 1, :]
                po[pl.ds(b * FR + f, 1), :] = own + moved * (1.0 / S)
        for l in range(L):
            send_buf[j, e, l] = acc_buf[pl.ds(l, FR, stride=L), :].astype(BF)
        recv_buf[j, e, :, rows(tm * FR, FR), :] = send_buf[j, e, rows(y * 8, 8)]

    def edge_pair(j):
        @pl.when(j == 1)
        def _():
            for side in range(2):
                pos_copy(side).wait()
            pt[:G] = pos_ghost[0]
            pt[G + NB :] = pos_ghost[1]

        @pl.when(j >= 1)
        def _():
            q = j - 1
            for side in range(2):
                halo_copy(side, q).wait_recv()
            for f in range(FR):
                ext[f, G - 1 - q] = ghost[0, q, f]
                ext[f, G + NB + q] = ghost[1, q, f]

        for e in range(2):
            edge_block(j, e, 6 - j if e == 0 else 7 + j)
            for d in (4, 5, 7, 6, 1, 3, 2):
                msg_copy(j, e, d).start()

    def spectral_part(j, blocks):
        n = 8 * len(blocks)
        for i, e in enumerate(blocks):
            for d in range(1, 8):
                msg_copy(j, e, d).wait_recv()
            for r in range(0, 8, 2):
                c2 = dot(
                    fwd[...],
                    jnp.concatenate([recv_buf[j, e, r], recv_buf[j, e, r + 1]], axis=1),
                )
                c = c2[:T] + c2[T:]
                at = (i * 8 + r) * T
                coef[at : at + T, :] = c[:, :H]
                coef[at + T : at + 2 * T, :] = c[:, H:]

        def mode(k, carry):
            re = coef[pl.ds(k, n, stride=T), :]
            im = coef[pl.ds(K + k, n, stride=T), :]
            lhs = jnp.concatenate(
                [jnp.concatenate([re, -im], axis=1), jnp.concatenate([im, re], axis=1)], axis=0
            ).astype(BF)
            w = jnp.concatenate([spec[0, k], spec[1, k]], axis=0)
            m = dot(lhs, w)
            mixed[rows(k * n, n), :] = m[:n]
            mixed[rows((K + k) * n, n), :] = m[n:]
            return carry

        lax.fori_loop(0, K, mode, 0, unroll=8)
        rows_t = rows(half * 64, 64)
        inv = jnp.concatenate([inv_hi[rows_t, :], inv_lo[rows_t, :]], axis=0)
        for i, e in enumerate(blocks):
            for r in range(0, 8, 2):
                m = jnp.concatenate(
                    [mixed[pl.ds(i * 8 + r + v, T, stride=n), :] for v in range(2)], axis=1
                )
                hi = m.astype(BF)
                lo = (m - hi.astype(F32)).astype(BF)
                c2 = dot(inv, hi)
                c = (c2[:64] + c2[64:] + dot(inv[:64], lo)).astype(BF)
                conv_buf[j, e, r] = c[:, :H]
                conv_buf[j, e, r + 1] = c[:, H:]
            for d in (2, 1, 3):
                conv_copy(j, e, d).start()
            back_buf[j, e, y] = conv_buf[j, e, :, rows(y * FR, FR), :]

    def node_pair(j):
        for e in range(2):
            b = 6 - j if e == 0 else 7 + j
            for d in (1, 3, 2):
                conv_copy(j, e, d).wait_recv()
            node_buf[...] = dot(back_buf[j, e].reshape(L * FR, H), w_n2[...])
            part = jnp.concatenate(
                [node_buf[pl.ds(f, L, stride=FR), :] for f in range(FR)], axis=0
            )
            own = own_all(b)
            pre = dot(own, w_n1[...]) + part + node_b0
            hidden = (pre * jnp.tanh(pre) + pre).astype(BF)
            res = own.astype(F32) + (dot(hidden, node_out[...]) + node_b1)
            res = res.astype(BF)
            for f in range(FR):
                out[f, rows(b * L, L), :] = res[f * L : (f + 1) * L]

    def close_sends(j, carry):
        for e in range(2):
            for d in range(1, 8):
                msg_copy(j, e, d).wait_send()
            for d in range(1, 4):
                conv_copy(j, e, d).wait_send()
        return carry

    def before_last():
        for d in range(3):
            for q in range(4):
                tile = jnp.zeros((FR, 128), F32)
                for w in range(4):
                    b = q * 4 + w
                    if b < NB:
                        part = po[b * FR : (b + 1) * FR, :]
                        shift = (L * (w - d)) % 128
                        if shift:
                            part = pltpu.roll(part, shift, 1)
                        tile = jnp.where(group16 == w, part, tile)
                width = min(128, NB * L - q * 128)
                out_pos[d, :, q * 128 : q * 128 + width] = tile[:, :width]
        for side in range(2):
            for q in range(G):
                halo_copy(side, q).wait_send()
        lax.fori_loop(0, PAIRS - 2, close_sends, 0)

    def step(j, carry):
        @pl.when(j < PAIRS)
        def _():
            edge_pair(j)

        @pl.when(j > LAG)
        def _():
            node_pair(j - LAG - 1)

        @pl.when(j == LAG)
        def _():
            spec_copy.wait()

        @pl.when((j >= LAG) & (j < PAIRS + LAG - 1))
        def _():
            spectral_part(j - LAG, (0, 1))

        return carry

    lax.fori_loop(0, PAIRS + LAG - 1, step, 0)
    last = PAIRS - 1
    node_pair(last - 1)
    before_last()
    spectral_part(last, (0,))
    spectral_part(last, (1,))
    node_pair(last)
    lax.fori_loop(PAIRS - 2, PAIRS, close_sends, 0)


def shards(
    node_feats,
    positions,
    neighbours,
    edge_in,
    edge_out,
    edge_params,
    coord_weight,
    spectral,
    node_in,
    node_out,
    node_bias,
):
    idx = jnp.transpose(neighbours, (1, 2, 0))
    pos3 = jnp.transpose(positions, (1, 0, 2))
    fwd, inv_hi, inv_lo = transforms()
    vmem = pl.BlockSpec(memory_space=pltpu.VMEM)
    hbm = pl.BlockSpec(memory_space=pl.ANY)
    dma = pltpu.SemaphoreType.DMA
    new_feats, pos_out = pl.pallas_call(
        kernel,
        out_shape=(
            pltpu.VMEM((FR, NB * L, H), BF),
            pltpu.VMEM((3, FR, NB * L), F32),
        ),
        in_specs=[pl.BlockSpec(memory_space=pltpu.SMEM)] + [vmem] * 11 + [hbm] * 2,
        out_specs=(vmem, vmem),
        scratch_shapes=[
            pltpu.VMEM((FR, EXT, L, H), BF),
            pltpu.VMEM((2, G, FR, L, H), BF),
            pltpu.VMEM((2, G, FR, 128), F32),
            pltpu.VMEM((EXT, FR, 128), F32),
            pltpu.VMEM((NB * FR, 128), F32),
            pltpu.VMEM((FR * S, 128), F32),
            pltpu.VMEM((FR * S, 128), F32),
            pltpu.VMEM((FR * L, H), F32),
            pltpu.VMEM((PAIRS, 2, L, FR, H), BF),
            pltpu.VMEM((PAIRS, 2, 8, T, H), BF),
            pltpu.VMEM((PAIRS, 2, 8, 64, H), BF),
            pltpu.VMEM((PAIRS, 2, 4, 8, FR, H), BF),
            pltpu.VMEM((2, K, H, H), BF),
            pltpu.VMEM((16 * T, H), F32),
            pltpu.VMEM((16 * T, H), F32),
            pltpu.VMEM((FR * L, H), F32),
            pltpu.VMEM((4, 2 * H, 2 * H), BF),
            pltpu.VMEM((2 * H, 2 * H), BF),
            pltpu.VMEM((2 * H, 2 * H), BF),
            pltpu.VMEM((4, 2 * H, H), BF),
            pltpu.VMEM((H, H), BF),
            pltpu.VMEM((H, H), BF),
            dma((2,)),
            dma((2,)),
            dma((2,)),
            dma((2, G)),
            dma((2, G)),
            dma((PAIRS, 2, 7)),
            dma((PAIRS, 2, 7)),
            dma((PAIRS, 2, 3)),
            dma((PAIRS, 2, 3)),
        ],
        compiler_params=pltpu.CompilerParams(
            collective_id=0, has_side_effects=True, vmem_limit_bytes=56 * 1024 * 1024
        ),
    )(
        idx,
        pos3,
        edge_in,
        edge_out,
        edge_params,
        coord_weight.reshape(1, H),
        node_in,
        node_out,
        node_bias,
        fwd,
        inv_hi,
        inv_lo,
        node_feats.reshape(FR, NB, L, H),
        spectral,
    )
    new_positions = jnp.transpose(pos_out, (1, 0, 2))
    return (new_feats, new_positions)


def solution(mesh):
    placed = (
        P("tm", "space", None),
        P("tm", None, "space"),
        P("tm", "space", None),
        P(),
        P(),
        P(),
        P(),
        P(),
        P(),
        P(),
        P(),
    )
    return jax.shard_map(
        shards,
        mesh=mesh,
        in_specs=placed,
        out_specs=(P("tm", "space", None), P("tm", None, "space")),
        check_vma=False,
    )
```

```python
import math

import jax
import jax.numpy as jnp
import numpy as np
from jax import lax
from jax.experimental import pallas as pl
from jax.experimental.pallas import tpu as pltpu
from jax.sharding import PartitionSpec as P

H = 128
L = 32
G = 6
FR = 16
NB = 14
EXT = NB + 2 * G
S = 8
T = 128
K = 64
PAIRS = 7
LAG = 1
MESH = pl.DeviceIdType.MESH
F32 = jnp.float32
BF = jnp.bfloat16


def dot(a, b):
    return jnp.dot(a, b, preferred_element_type=F32)


def split_np(values):
    import ml_dtypes

    high = values.astype(ml_dtypes.bfloat16)
    low = (values - high.astype(np.float64)).astype(ml_dtypes.bfloat16)
    return high, low


def transforms():
    k = np.arange(K)
    t = np.arange(T)
    angle = 2.0 * math.pi / T * ((k[:, None] * t[None, :]) % T)
    forward = np.concatenate([np.cos(angle), -np.sin(angle)], axis=0)
    fwd = np.concatenate(split_np(forward), axis=0)
    weight = (np.where(k == 0, 1.0, 2.0) / T)[None, :]
    inverse = np.concatenate([np.cos(angle.T) * weight, -np.sin(angle.T) * weight], axis=1)
    inv_hi, inv_lo = split_np(inverse)
    return jnp.asarray(fwd), jnp.asarray(inv_hi), jnp.asarray(inv_lo)


def rows(start, size):
    return pl.ds(pl.multiple_of(start, size), size)


def kernel(
    idx,
    pos3,
    edge_in,
    edge_out,
    edge_params,
    coord_w,
    node_in,
    node_out,
    node_bias,
    fwd,
    inv_hi,
    inv_lo,
    feats_hbm,
    spec_hbm,
    out,
    out_pos,
    ext,
    ghost,
    pos_ghost,
    pt,
    po,
    near,
    scaled,
    acc_buf,
    send_buf,
    recv_buf,
    conv_buf,
    back_buf,
    spec,
    coef,
    mixed,
    node_buf,
    w_src,
    w_dst,
    w_edge,
    w_coord,
    w_n1,
    w_n2,
    loc_sem,
    pos_send,
    pos_recv,
    halo_send,
    halo_recv,
    msg_send,
    msg_recv,
    conv_send,
    conv_recv,
):
    sp = lax.axis_index("space")
    tm = lax.axis_index("tm")
    count = lax.axis_size("space")
    y = tm % 4
    half = tm // 4
    total = NB * count
    first_block = sp * NB - G
    right = (sp + 1) % count
    left = (sp + count - 1) % count

    def partner_y(d):
        if d % 4 == 0:
            return y
        if d % 4 == 1:
            return y + 1 - 2 * (y % 2)
        if d % 4 == 2:
            return (y + 2) % 4
        return 3 - y

    def partner(d):
        return (1 - half if d >= 4 else half) * 4 + partner_y(d)

    barrier = pltpu.get_barrier_semaphore()
    for other in (left, right):
        pl.semaphore_signal(barrier, inc=1, device_id=(other, tm), device_id_type=MESH)
    for d in range(1, 8):
        pl.semaphore_signal(barrier, inc=1, device_id=(sp, partner(d)), device_id_type=MESH)

    own_copy = pltpu.make_async_copy(feats_hbm, ext.at[:, pl.ds(G, NB)], loc_sem.at[0])
    own_copy.start()
    spec_copy = pltpu.make_async_copy(spec_hbm, spec, loc_sem.at[1])
    spec_copy.start()

    pl.semaphore_wait(barrier, 9)

    def pos_copy(side):
        if side == 0:
            src, dev = NB, right
        else:
            src, dev = G, left
        return pltpu.make_async_remote_copy(
            src_ref=pt.at[pl.ds(src, G)],
            dst_ref=pos_ghost.at[side],
            send_sem=pos_send.at[side],
            recv_sem=pos_recv.at[side],
            device_id=(dev, tm),
            device_id_type=MESH,
        )

    def halo_copy(side, q):
        if side == 0:
            src, dev = NB - 1 - q, right
        else:
            src, dev = q, left
        return pltpu.make_async_remote_copy(
            src_ref=feats_hbm.at[:, src],
            dst_ref=ghost.at[side, q],
            send_sem=halo_send.at[side, q],
            recv_sem=halo_recv.at[side, q],
            device_id=(dev, tm),
            device_id_type=MESH,
        )

    def msg_copy(j, e, d):
        return pltpu.make_async_remote_copy(
            src_ref=send_buf.at[j, e, rows(partner_y(d) * 8, 8)],
            dst_ref=recv_buf.at[j, e, :, rows(tm * FR, FR), :],
            send_sem=msg_send.at[j, e, d - 1],
            recv_sem=msg_recv.at[j, e, d - 1],
            device_id=(sp, partner(d)),
            device_id_type=MESH,
        )

    def conv_copy(j, e, d):
        return pltpu.make_async_remote_copy(
            src_ref=conv_buf.at[j, e, :, rows(partner_y(d) * FR, FR), :],
            dst_ref=back_buf.at[j, e, y],
            send_sem=conv_send.at[j, e, d - 1],
            recv_sem=conv_recv.at[j, e, d - 1],
            device_id=(sp, partner(d)),
            device_id_type=MESH,
        )

    for side in range(2):
        halo_copy(side, 0).start()

    group16 = lax.broadcasted_iota(jnp.int32, (FR, 128), 1) // L
    for b in range(NB):
        q, w = b // 4, b % 4
        tile = jnp.zeros((FR, 128), F32)
        for d in range(3):
            if q < 3:
                part = pos3[d, :, q * 128 : (q + 1) * 128]
            else:
                part = jnp.concatenate(
                    [pos3[d, :, 384:448], jnp.zeros((FR, 64), F32)], axis=1
                )
            shift = (L * (d - w)) % 128
            if shift:
                part = pltpu.roll(part, shift, 1)
            tile = jnp.where(group16 == d, part, tile)
        pt[G + b] = tile

    for side in range(2):
        pos_copy(side).start()
    for q in range(1, G):
        for side in range(2):
            halo_copy(side, q).start()

    def half_bf(v):
        return (v.astype(F32) * 0.5).astype(BF)

    zero = jnp.zeros((H, H), BF)
    src_half = half_bf(edge_in[:H, :])
    dst_half = half_bf(edge_in[H:, :])
    edge_half = half_bf(edge_out[...])
    row = lax.broadcasted_iota(jnp.int32, (H, H), 0)
    lane = lax.broadcasted_iota(jnp.int32, (H, H), 1)
    bias = edge_params[0:1, :] * 0.5
    dist_w = edge_params[1:2, :] * 0.5

    def split3(v):
        a = v.astype(BF).astype(F32)
        r = v - a
        b = r.astype(BF).astype(F32)
        return a, b, (r - b).astype(BF).astype(F32)

    bias_parts = split3(bias)
    dist_hi, dist_lo, _ = split3(dist_w)
    cw_hi = jnp.broadcast_to(coord_w[...], (H, H)).T
    cw_hi, cw_lo, _ = split3(cw_hi)
    for s in range(S):
        p, c = s // 2, (s % 2) * H
        w_src[p, :H, c : c + H] = src_half
        block = jnp.where((row == s) | (row == 8 + s), dist_hi, 0.0)
        block = jnp.where(row == 16 + s, dist_lo, block)
        for i in range(3):
            block = jnp.where(row == 24 + i, bias_parts[i], block)
        w_src[p, H:, c : c + H] = block.astype(BF)
        w_coord[p, c : c + H, :] = jnp.where(
            lane == s, cw_hi, jnp.where(lane == 8 + s, cw_lo, 0.0)
        ).astype(BF)
    for dst_ref, w in ((w_dst, dst_half), (w_edge, edge_half)):
        dst_ref[:H, :H] = w
        dst_ref[H:, H:] = w
        dst_ref[:H, H:] = zero
        dst_ref[H:, :H] = zero
    w_n1[...] = half_bf(node_in[:H, :])
    w_n2[...] = half_bf(node_in[H:, :])
    edge_bias = edge_params[2:3, :] * 0.5
    edge_bias2 = jnp.concatenate([edge_bias, edge_bias], axis=1)
    node_b0 = node_bias[0:1, :] * 0.5
    node_b1 = node_bias[1:2, :]

    own_copy.wait()

    group = lax.broadcasted_iota(jnp.int32, (8, 128), 1) // L

    def own_all(b):
        return jnp.concatenate([ext[f, G + b] for f in range(FR)], axis=0)

    def edge_block(j, e, b):
        picked = {}
        for f in range(FR):
            for s in range(S):
                v = idx[b, s, f] - first_block
                v = jnp.where(v < 0, v + total, v)
                v = jnp.where(v >= total, v - total, v)
                picked[f, s] = jnp.minimum(v, EXT - 1)
        augs = []
        for h in range(4):
            dist = jnp.zeros((8, 128), F32)
            for u in range(4):
                f = h * 4 + u
                for s in range(S):
                    near[f * 8 + s : f * 8 + s + 1, :] = pt[picked[f, s], f : f + 1, :]
                own = pt[G + b, f : f + 1, :]
                offset = own - near[f * 8 : (f + 1) * 8, :]
                square = offset * offset
                square = square + pltpu.roll(square, 64, 1)
                square = square + pltpu.roll(square, 32, 1)
                scaled[f * 8 : (f + 1) * 8, :] = offset / (1.0 + jnp.sqrt(square + 1.0))
                dist = jnp.where(group == u, square, dist)
            d_hi = dist.astype(BF).astype(F32)
            d_lo = (dist - d_hi).astype(BF).astype(F32)
            aug = jnp.concatenate(
                [d_hi, d_lo, d_hi, jnp.ones((8, 128), F32), jnp.zeros((96, 128), F32)], axis=0
            )
            augs.append(aug.T.astype(BF))
        first = jnp.concatenate([own_all(b), jnp.concatenate(augs, axis=0)], axis=1)
        acc = None
        wsum = None
        for p in range(4):
            cols = []
            for s in (2 * p, 2 * p + 1):
                cols.append(
                    jnp.concatenate(
                        [ext[f, picked[f, s]] for f in range(FR)], axis=0
                    )
                )
            second = jnp.concatenate(cols, axis=1)
            pre = dot(first, w_src[p]) + dot(second, w_dst[...])
            hidden = (pre * jnp.tanh(pre) + pre).astype(BF)
            act = dot(hidden, w_edge[...]) + edge_bias2
            msg = act * jnp.tanh(act) + act
            both = msg[:, :H] + msg[:, H:]
            part = dot(msg.astype(BF), w_coord[p])
            acc = both if p == 0 else acc + both
            wsum = part if p == 0 else wsum + part
        acc_buf[...] = acc * (1.0 / S)
        for h in range(4):
            wt = wsum[h * 128 : (h + 1) * 128, :].T
            wv = wt[0:8, :] + wt[8:16, :]
            for u in range(4):
                f = h * 4 + u
                one = jnp.where(group == u, wv, 0.0)
                one = one + pltpu.roll(one, 64, 1)
                one = one + pltpu.roll(one, 32, 1)
                moved = jnp.sum(scaled[f * 8 : (f + 1) * 8, :] * one, axis=0, keepdims=True)
                own = pt[G + b, f : f + 1, :]
                po[pl.ds(b * FR + f, 1), :] = own + moved * (1.0 / S)
        for l in range(L):
            send_buf[j, e, l] = acc_buf[pl.ds(l, FR, stride=L), :].astype(BF)
        recv_buf[j, e, :, rows(tm * FR, FR), :] = send_buf[j, e, rows(y * 8, 8)]

    def edge_pair(j):
        @pl.when(j == 1)
        def _():
            for side in range(2):
                pos_copy(side).wait()
            for e in range(2):
                for d in (4, 5, 7, 6, 1, 3, 2):
                    msg_copy(0, e, d).start()
            pt[:G] = pos_ghost[0]
            pt[G + NB :] = pos_ghost[1]

        @pl.when(j >= 1)
        def _():
            q = j - 1
            for side in range(2):
                halo_copy(side, q).wait_recv()
            for f in range(FR):
                ext[f, G - 1 - q] = ghost[0, q, f]
                ext[f, G + NB + q] = ghost[1, q, f]

        for e in range(2):
            edge_block(j, e, 6 - j if e == 0 else 7 + j)
            @pl.when(j > 0)
            def _():
                for d in (4, 5, 7, 6, 1, 3, 2):
                    msg_copy(j, e, d).start()

    def spectral_part(j, blocks):
        n = 8 * len(blocks)
        for i, e in enumerate(blocks):
            for d in range(1, 8):
                msg_copy(j, e, d).wait_recv()
            for r in range(0, 8, 2):
                c2 = dot(
                    fwd[...],
                    jnp.concatenate([recv_buf[j, e, r], recv_buf[j, e, r + 1]], axis=1),
                )
                c = c2[:T] + c2[T:]
                at = (i * 8 + r) * T
                coef[at : at + T, :] = c[:, :H]
                coef[at + T : at + 2 * T, :] = c[:, H:]

        def mode(k, carry):
            re = coef[pl.ds(k, n, stride=T), :]
            im = coef[pl.ds(K + k, n, stride=T), :]
            lhs = jnp.concatenate(
                [jnp.concatenate([re, -im], axis=1), jnp.concatenate([im, re], axis=1)], axis=0
            ).astype(BF)
            w = jnp.concatenate([spec[0, k], spec[1, k]], axis=0)
            m = dot(lhs, w)
            mixed[rows(k * n, n), :] = m[:n]
            mixed[rows((K + k) * n, n), :] = m[n:]
            return carry

        lax.fori_loop(0, K, mode, 0, unroll=8)
        rows_t = rows(half * 64, 64)
        inv = jnp.concatenate([inv_hi[rows_t, :], inv_lo[rows_t, :]], axis=0)
        for i, e in enumerate(blocks):
            for r in range(0, 8, 2):
                m = jnp.concatenate(
                    [mixed[pl.ds(i * 8 + r + v, T, stride=n), :] for v in range(2)], axis=1
                )
                hi = m.astype(BF)
                lo = (m - hi.astype(F32)).astype(BF)
                c2 = dot(inv, hi)
                c = (c2[:64] + c2[64:] + dot(inv[:64], lo)).astype(BF)
                conv_buf[j, e, r] = c[:, :H]
                conv_buf[j, e, r + 1] = c[:, H:]
            for d in (2, 1, 3):
                conv_copy(j, e, d).start()
            back_buf[j, e, y] = conv_buf[j, e, :, rows(y * FR, FR), :]

    def node_pair(j):
        for e in range(2):
            b = 6 - j if e == 0 else 7 + j
            for d in (1, 3, 2):
                conv_copy(j, e, d).wait_recv()
            node_buf[...] = dot(back_buf[j, e].reshape(L * FR, H), w_n2[...])
            part = jnp.concatenate(
                [node_buf[pl.ds(f, L, stride=FR), :] for f in range(FR)], axis=0
            )
            own = own_all(b)
            pre = dot(own, w_n1[...]) + part + node_b0
            hidden = (pre * jnp.tanh(pre) + pre).astype(BF)
            res = own.astype(F32) + (dot(hidden, node_out[...]) + node_b1)
            res = res.astype(BF)
            for f in range(FR):
                out[f, rows(b * L, L), :] = res[f * L : (f + 1) * L]

    def close_sends(j, carry):
        for e in range(2):
            for d in range(1, 8):
                msg_copy(j, e, d).wait_send()
            for d in range(1, 4):
                conv_copy(j, e, d).wait_send()
        return carry

    def before_last():
        for d in range(3):
            for q in range(4):
                tile = jnp.zeros((FR, 128), F32)
                for w in range(4):
                    b = q * 4 + w
                    if b < NB:
                        part = po[b * FR : (b + 1) * FR, :]
                        shift = (L * (w - d)) % 128
                        if shift:
                            part = pltpu.roll(part, shift, 1)
                        tile = jnp.where(group16 == w, part, tile)
                width = min(128, NB * L - q * 128)
                out_pos[d, :, q * 128 : q * 128 + width] = tile[:, :width]
        for side in range(2):
            for q in range(G):
                halo_copy(side, q).wait_send()
        lax.fori_loop(0, PAIRS - 2, close_sends, 0)

    def step(j, carry):
        @pl.when(j < PAIRS)
        def _():
            edge_pair(j)

        @pl.when(j > LAG)
        def _():
            node_pair(j - LAG - 1)

        @pl.when(j == LAG)
        def _():
            spec_copy.wait()

        @pl.when((j >= LAG) & (j < PAIRS + LAG - 1))
        def _():
            spectral_part(j - LAG, (0, 1))

        return carry

    lax.fori_loop(0, PAIRS + LAG - 1, step, 0)
    last = PAIRS - 1
    node_pair(last - 1)
    before_last()
    spectral_part(last, (0,))
    spectral_part(last, (1,))
    node_pair(last)
    lax.fori_loop(PAIRS - 2, PAIRS, close_sends, 0)


def shards(
    node_feats,
    positions,
    neighbours,
    edge_in,
    edge_out,
    edge_params,
    coord_weight,
    spectral,
    node_in,
    node_out,
    node_bias,
):
    idx = jnp.transpose(neighbours, (1, 2, 0))
    pos3 = jnp.transpose(positions, (1, 0, 2))
    fwd, inv_hi, inv_lo = transforms()
    vmem = pl.BlockSpec(memory_space=pltpu.VMEM)
    hbm = pl.BlockSpec(memory_space=pl.ANY)
    dma = pltpu.SemaphoreType.DMA
    new_feats, pos_out = pl.pallas_call(
        kernel,
        out_shape=(
            pltpu.VMEM((FR, NB * L, H), BF),
            pltpu.VMEM((3, FR, NB * L), F32),
        ),
        in_specs=[pl.BlockSpec(memory_space=pltpu.SMEM)] + [vmem] * 11 + [hbm] * 2,
        out_specs=(vmem, vmem),
        scratch_shapes=[
            pltpu.VMEM((FR, EXT, L, H), BF),
            pltpu.VMEM((2, G, FR, L, H), BF),
            pltpu.VMEM((2, G, FR, 128), F32),
            pltpu.VMEM((EXT, FR, 128), F32),
            pltpu.VMEM((NB * FR, 128), F32),
            pltpu.VMEM((FR * S, 128), F32),
            pltpu.VMEM((FR * S, 128), F32),
            pltpu.VMEM((FR * L, H), F32),
            pltpu.VMEM((PAIRS, 2, L, FR, H), BF),
            pltpu.VMEM((PAIRS, 2, 8, T, H), BF),
            pltpu.VMEM((PAIRS, 2, 8, 64, H), BF),
            pltpu.VMEM((PAIRS, 2, 4, 8, FR, H), BF),
            pltpu.VMEM((2, K, H, H), BF),
            pltpu.VMEM((16 * T, H), F32),
            pltpu.VMEM((16 * T, H), F32),
            pltpu.VMEM((FR * L, H), F32),
            pltpu.VMEM((4, 2 * H, 2 * H), BF),
            pltpu.VMEM((2 * H, 2 * H), BF),
            pltpu.VMEM((2 * H, 2 * H), BF),
            pltpu.VMEM((4, 2 * H, H), BF),
            pltpu.VMEM((H, H), BF),
            pltpu.VMEM((H, H), BF),
            dma((2,)),
            dma((2,)),
            dma((2,)),
            dma((2, G)),
            dma((2, G)),
            dma((PAIRS, 2, 7)),
            dma((PAIRS, 2, 7)),
            dma((PAIRS, 2, 3)),
            dma((PAIRS, 2, 3)),
        ],
        compiler_params=pltpu.CompilerParams(
            collective_id=0, has_side_effects=True, vmem_limit_bytes=56 * 1024 * 1024
        ),
    )(
        idx,
        pos3,
        edge_in,
        edge_out,
        edge_params,
        coord_weight.reshape(1, H),
        node_in,
        node_out,
        node_bias,
        fwd,
        inv_hi,
        inv_lo,
        node_feats.reshape(FR, NB, L, H),
        spectral,
    )
    new_positions = jnp.transpose(pos_out, (1, 0, 2))
    return (new_feats, new_positions)


def solution(mesh):
    placed = (
        P("tm", "space", None),
        P("tm", None, "space"),
        P("tm", "space", None),
        P(),
        P(),
        P(),
        P(),
        P(),
        P(),
        P(),
        P(),
    )
    return jax.shard_map(
        shards,
        mesh=mesh,
        in_specs=placed,
        out_specs=(P("tm", "space", None), P("tm", None, "space")),
        check_vma=False,
    )
```

```python
import math

import jax
import jax.numpy as jnp
import numpy as np
from jax import lax
from jax.experimental import pallas as pl
from jax.experimental.pallas import tpu as pltpu
from jax.sharding import PartitionSpec as P

H = 128
L = 32
G = 6
FR = 16
NB = 14
EXT = NB + 2 * G
S = 8
T = 128
K = 64
PAIRS = 7
LAG = 1
MESH = pl.DeviceIdType.MESH
F32 = jnp.float32
BF = jnp.bfloat16


def dot(a, b):
    return jnp.dot(a, b, preferred_element_type=F32)


def split_np(values):
    import ml_dtypes

    high = values.astype(ml_dtypes.bfloat16)
    low = (values - high.astype(np.float64)).astype(ml_dtypes.bfloat16)
    return high, low


def transforms():
    k = np.arange(K)
    t = np.arange(T)
    angle = 2.0 * math.pi / T * ((k[:, None] * t[None, :]) % T)
    forward = np.concatenate([np.cos(angle), -np.sin(angle)], axis=0)
    fwd = np.concatenate(split_np(forward), axis=0)
    weight = (np.where(k == 0, 1.0, 2.0) / T)[None, :]
    inverse = np.concatenate([np.cos(angle.T) * weight, -np.sin(angle.T) * weight], axis=1)
    inv_hi, inv_lo = split_np(inverse)
    return jnp.asarray(fwd), jnp.asarray(inv_hi), jnp.asarray(inv_lo)


def rows(start, size):
    return pl.ds(pl.multiple_of(start, size), size)


def kernel(
    idx,
    pos3,
    edge_in,
    edge_out,
    edge_params,
    coord_w,
    node_in,
    node_out,
    node_bias,
    fwd,
    inv_hi,
    inv_lo,
    feats_hbm,
    spec_hbm,
    out,
    out_pos,
    ext,
    ghost,
    pos_ghost,
    pt,
    po,
    near,
    scaled,
    acc_buf,
    send_buf,
    recv_buf,
    conv_buf,
    back_buf,
    spec,
    coef,
    mixed,
    node_buf,
    w_src,
    w_dst,
    w_edge,
    w_coord,
    w_n1,
    w_n2,
    loc_sem,
    pos_send,
    pos_recv,
    halo_send,
    halo_recv,
    msg_send,
    msg_recv,
    conv_send,
    conv_recv,
):
    sp = lax.axis_index("space")
    tm = lax.axis_index("tm")
    count = lax.axis_size("space")
    y = tm % 4
    half = tm // 4
    total = NB * count
    first_block = sp * NB - G
    right = (sp + 1) % count
    left = (sp + count - 1) % count

    def partner_y(d):
        if d % 4 == 0:
            return y
        if d % 4 == 1:
            return y + 1 - 2 * (y % 2)
        if d % 4 == 2:
            return (y + 2) % 4
        return 3 - y

    def partner(d):
        return (1 - half if d >= 4 else half) * 4 + partner_y(d)

    barrier = pltpu.get_barrier_semaphore()
    for other in (left, right):
        pl.semaphore_signal(barrier, inc=1, device_id=(other, tm), device_id_type=MESH)
    for d in range(1, 8):
        pl.semaphore_signal(barrier, inc=1, device_id=(sp, partner(d)), device_id_type=MESH)

    own_copy = pltpu.make_async_copy(feats_hbm, ext.at[:, pl.ds(G, NB)], loc_sem.at[0])
    own_copy.start()
    spec_copy = pltpu.make_async_copy(spec_hbm, spec, loc_sem.at[1])
    spec_copy.start()

    pl.semaphore_wait(barrier, 9)

    def pos_copy(side):
        if side == 0:
            src, dev = NB, right
        else:
            src, dev = G, left
        return pltpu.make_async_remote_copy(
            src_ref=pt.at[pl.ds(src, G)],
            dst_ref=pos_ghost.at[side],
            send_sem=pos_send.at[side],
            recv_sem=pos_recv.at[side],
            device_id=(dev, tm),
            device_id_type=MESH,
        )

    def halo_copy(side, q):
        if side == 0:
            src, dev = NB - 1 - q, right
        else:
            src, dev = q, left
        return pltpu.make_async_remote_copy(
            src_ref=feats_hbm.at[:, src],
            dst_ref=ghost.at[side, q],
            send_sem=halo_send.at[side, q],
            recv_sem=halo_recv.at[side, q],
            device_id=(dev, tm),
            device_id_type=MESH,
        )

    def msg_copy(j, e, d):
        return pltpu.make_async_remote_copy(
            src_ref=send_buf.at[j, e, rows(partner_y(d) * 8, 8)],
            dst_ref=recv_buf.at[j, e, :, rows(tm * FR, FR), :],
            send_sem=msg_send.at[j, e, d - 1],
            recv_sem=msg_recv.at[j, e, d - 1],
            device_id=(sp, partner(d)),
            device_id_type=MESH,
        )

    def conv_copy(j, e, d):
        return pltpu.make_async_remote_copy(
            src_ref=conv_buf.at[j, e, :, rows(partner_y(d) * FR, FR), :],
            dst_ref=back_buf.at[j, e, y],
            send_sem=conv_send.at[j, e, d - 1],
            recv_sem=conv_recv.at[j, e, d - 1],
            device_id=(sp, partner(d)),
            device_id_type=MESH,
        )

    for side in range(2):
        halo_copy(side, 0).start()

    group16 = lax.broadcasted_iota(jnp.int32, (FR, 128), 1) // L
    for b in range(NB):
        q, w = b // 4, b % 4
        tile = jnp.zeros((FR, 128), F32)
        for d in range(3):
            if q < 3:
                part = pos3[d, :, q * 128 : (q + 1) * 128]
            else:
                part = jnp.concatenate(
                    [pos3[d, :, 384:448], jnp.zeros((FR, 64), F32)], axis=1
                )
            shift = (L * (d - w)) % 128
            if shift:
                part = pltpu.roll(part, shift, 1)
            tile = jnp.where(group16 == d, part, tile)
        pt[G + b] = tile

    for side in range(2):
        pos_copy(side).start()
    for q in range(1, G):
        for side in range(2):
            halo_copy(side, q).start()

    def half_bf(v):
        return (v.astype(F32) * 0.5).astype(BF)

    zero = jnp.zeros((H, H), BF)
    src_half = half_bf(edge_in[:H, :])
    dst_half = half_bf(edge_in[H:, :])
    edge_half = half_bf(edge_out[...])
    row = lax.broadcasted_iota(jnp.int32, (H, H), 0)
    lane = lax.broadcasted_iota(jnp.int32, (H, H), 1)
    bias = edge_params[0:1, :] * 0.5
    dist_w = edge_params[1:2, :] * 0.5

    def split3(v):
        a = v.astype(BF).astype(F32)
        r = v - a
        b = r.astype(BF).astype(F32)
        return a, b, (r - b).astype(BF).astype(F32)

    bias_parts = split3(bias)
    dist_hi, dist_lo, _ = split3(dist_w)
    cw_hi = jnp.broadcast_to(coord_w[...], (H, H)).T
    cw_hi, cw_lo, _ = split3(cw_hi)
    for s in range(S):
        p, c = s // 2, (s % 2) * H
        w_src[p, :H, c : c + H] = src_half
        block = jnp.where((row == s) | (row == 8 + s), dist_hi, 0.0)
        block = jnp.where(row == 16 + s, dist_lo, block)
        for i in range(3):
            block = jnp.where(row == 24 + i, bias_parts[i], block)
        w_src[p, H:, c : c + H] = block.astype(BF)
        w_coord[p, c : c + H, :] = jnp.where(
            lane == s, cw_hi, jnp.where(lane == 8 + s, cw_lo, 0.0)
        ).astype(BF)
    for dst_ref, w in ((w_dst, dst_half), (w_edge, edge_half)):
        dst_ref[:H, :H] = w
        dst_ref[H:, H:] = w
        dst_ref[:H, H:] = zero
        dst_ref[H:, :H] = zero
    w_n1[...] = half_bf(node_in[:H, :])
    w_n2[...] = half_bf(node_in[H:, :])
    edge_bias = edge_params[2:3, :] * 0.5
    edge_bias2 = jnp.concatenate([edge_bias, edge_bias], axis=1)
    node_b0 = node_bias[0:1, :] * 0.5
    node_b1 = node_bias[1:2, :]

    own_copy.wait()

    group = lax.broadcasted_iota(jnp.int32, (8, 128), 1) // L

    def own_all(b):
        return jnp.concatenate([ext[f, G + b] for f in range(FR)], axis=0)

    def edge_block(j, e, b):
        picked = {}
        for f in range(FR):
            for s in range(S):
                v = idx[b, s, f] - first_block
                v = jnp.where(v < 0, v + total, v)
                v = jnp.where(v >= total, v - total, v)
                picked[f, s] = jnp.minimum(v, EXT - 1)
        augs = []
        for h in range(4):
            dist = jnp.zeros((8, 128), F32)
            for u in range(4):
                f = h * 4 + u
                for s in range(S):
                    near[f * 8 + s : f * 8 + s + 1, :] = pt[picked[f, s], f : f + 1, :]
                own = pt[G + b, f : f + 1, :]
                offset = own - near[f * 8 : (f + 1) * 8, :]
                square = offset * offset
                square = square + pltpu.roll(square, 64, 1)
                square = square + pltpu.roll(square, 32, 1)
                scaled[f * 8 : (f + 1) * 8, :] = offset / (1.0 + jnp.sqrt(square + 1.0))
                dist = jnp.where(group == u, square, dist)
            d_hi = dist.astype(BF).astype(F32)
            d_lo = (dist - d_hi).astype(BF).astype(F32)
            aug = jnp.concatenate(
                [d_hi, d_lo, d_hi, jnp.ones((8, 128), F32), jnp.zeros((96, 128), F32)], axis=0
            )
            augs.append(aug.T.astype(BF))
        first = jnp.concatenate([own_all(b), jnp.concatenate(augs, axis=0)], axis=1)
        acc = None
        wsum = None
        for p in range(4):
            cols = []
            for s in (2 * p, 2 * p + 1):
                cols.append(
                    jnp.concatenate(
                        [ext[f, picked[f, s]] for f in range(FR)], axis=0
                    )
                )
            second = jnp.concatenate(cols, axis=1)
            pre = dot(first, w_src[p]) + dot(second, w_dst[...])
            hidden = (pre * jnp.tanh(pre) + pre).astype(BF)
            act = dot(hidden, w_edge[...]) + edge_bias2
            msg = act * jnp.tanh(act) + act
            both = msg[:, :H] + msg[:, H:]
            part = dot(msg.astype(BF), w_coord[p])
            acc = both if p == 0 else acc + both
            wsum = part if p == 0 else wsum + part
        acc_buf[...] = acc * (1.0 / S)
        for h in range(4):
            wt = wsum[h * 128 : (h + 1) * 128, :].T
            wv = wt[0:8, :] + wt[8:16, :]
            for u in range(4):
                f = h * 4 + u
                one = jnp.where(group == u, wv, 0.0)
                one = one + pltpu.roll(one, 64, 1)
                one = one + pltpu.roll(one, 32, 1)
                moved = jnp.sum(scaled[f * 8 : (f + 1) * 8, :] * one, axis=0, keepdims=True)
                own = pt[G + b, f : f + 1, :]
                po[pl.ds(b * FR + f, 1), :] = own + moved * (1.0 / S)
        for l in range(L):
            send_buf[j, e, l] = acc_buf[pl.ds(l, FR, stride=L), :].astype(BF)
        recv_buf[j, e, :, rows(tm * FR, FR), :] = send_buf[j, e, rows(y * 8, 8)]

    def edge_pair(j):
        @pl.when(j == 1)
        def _():
            for side in range(2):
                pos_copy(side).wait()
            pt[:G] = pos_ghost[0]
            pt[G + NB :] = pos_ghost[1]

        @pl.when(j >= 1)
        def _():
            q = j - 1
            for side in range(2):
                halo_copy(side, q).wait_recv()
            for f in range(FR):
                ext[f, G - 1 - q] = ghost[0, q, f]
                ext[f, G + NB + q] = ghost[1, q, f]

        @pl.when(j == 1)
        def _():
            for e in range(2):
                for d in (4, 5, 7, 6, 1, 3, 2):
                    msg_copy(0, e, d).start()

        for e in range(2):
            edge_block(j, e, 6 - j if e == 0 else 7 + j)
            @pl.when(j > 0)
            def _():
                for d in (4, 5, 7, 6, 1, 3, 2):
                    msg_copy(j, e, d).start()

    def spectral_part(j, blocks):
        n = 8 * len(blocks)
        for i, e in enumerate(blocks):
            for d in range(1, 8):
                msg_copy(j, e, d).wait_recv()
            for r in range(0, 8, 2):
                c2 = dot(
                    fwd[...],
                    jnp.concatenate([recv_buf[j, e, r], recv_buf[j, e, r + 1]], axis=1),
                )
                c = c2[:T] + c2[T:]
                at = (i * 8 + r) * T
                coef[at : at + T, :] = c[:, :H]
                coef[at + T : at + 2 * T, :] = c[:, H:]

        def mode(k, carry):
            re = coef[pl.ds(k, n, stride=T), :]
            im = coef[pl.ds(K + k, n, stride=T), :]
            lhs = jnp.concatenate(
                [jnp.concatenate([re, -im], axis=1), jnp.concatenate([im, re], axis=1)], axis=0
            ).astype(BF)
            w = jnp.concatenate([spec[0, k], spec[1, k]], axis=0)
            m = dot(lhs, w)
            mixed[rows(k * n, n), :] = m[:n]
            mixed[rows((K + k) * n, n), :] = m[n:]
            return carry

        lax.fori_loop(0, K, mode, 0, unroll=8)
        rows_t = rows(half * 64, 64)
        inv = jnp.concatenate([inv_hi[rows_t, :], inv_lo[rows_t, :]], axis=0)
        for i, e in enumerate(blocks):
            for r in range(0, 8, 2):
                m = jnp.concatenate(
                    [mixed[pl.ds(i * 8 + r + v, T, stride=n), :] for v in range(2)], axis=1
                )
                hi = m.astype(BF)
                lo = (m - hi.astype(F32)).astype(BF)
                c2 = dot(inv, hi)
                c = (c2[:64] + c2[64:] + dot(inv[:64], lo)).astype(BF)
                conv_buf[j, e, r] = c[:, :H]
                conv_buf[j, e, r + 1] = c[:, H:]
            for d in (2, 1, 3):
                conv_copy(j, e, d).start()
            back_buf[j, e, y] = conv_buf[j, e, :, rows(y * FR, FR), :]

    def node_pair(j):
        for e in range(2):
            b = 6 - j if e == 0 else 7 + j
            for d in (1, 3, 2):
                conv_copy(j, e, d).wait_recv()
            node_buf[...] = dot(back_buf[j, e].reshape(L * FR, H), w_n2[...])
            part = jnp.concatenate(
                [node_buf[pl.ds(f, L, stride=FR), :] for f in range(FR)], axis=0
            )
            own = own_all(b)
            pre = dot(own, w_n1[...]) + part + node_b0
            hidden = (pre * jnp.tanh(pre) + pre).astype(BF)
            res = own.astype(F32) + (dot(hidden, node_out[...]) + node_b1)
            res = res.astype(BF)
            for f in range(FR):
                out[f, rows(b * L, L), :] = res[f * L : (f + 1) * L]

    def close_sends(j, carry):
        for e in range(2):
            for d in range(1, 8):
                msg_copy(j, e, d).wait_send()
            for d in range(1, 4):
                conv_copy(j, e, d).wait_send()
        return carry

    def before_last():
        for d in range(3):
            for q in range(4):
                tile = jnp.zeros((FR, 128), F32)
                for w in range(4):
                    b = q * 4 + w
                    if b < NB:
                        part = po[b * FR : (b + 1) * FR, :]
                        shift = (L * (w - d)) % 128
                        if shift:
                            part = pltpu.roll(part, shift, 1)
                        tile = jnp.where(group16 == w, part, tile)
                width = min(128, NB * L - q * 128)
                out_pos[d, :, q * 128 : q * 128 + width] = tile[:, :width]
        for side in range(2):
            for q in range(G):
                halo_copy(side, q).wait_send()
        lax.fori_loop(0, PAIRS - 2, close_sends, 0)

    def step(j, carry):
        @pl.when(j < PAIRS)
        def _():
            edge_pair(j)

        @pl.when(j > LAG)
        def _():
            node_pair(j - LAG - 1)

        @pl.when(j == LAG)
        def _():
            spec_copy.wait()

        @pl.when((j >= LAG) & (j < PAIRS + LAG - 1))
        def _():
            spectral_part(j - LAG, (0, 1))

        return carry

    lax.fori_loop(0, PAIRS + LAG - 1, step, 0)
    last = PAIRS - 1
    node_pair(last - 1)
    before_last()
    spectral_part(last, (0,))
    spectral_part(last, (1,))
    node_pair(last)
    lax.fori_loop(PAIRS - 2, PAIRS, close_sends, 0)


def shards(
    node_feats,
    positions,
    neighbours,
    edge_in,
    edge_out,
    edge_params,
    coord_weight,
    spectral,
    node_in,
    node_out,
    node_bias,
):
    idx = jnp.transpose(neighbours, (1, 2, 0))
    pos3 = jnp.transpose(positions, (1, 0, 2))
    fwd, inv_hi, inv_lo = transforms()
    vmem = pl.BlockSpec(memory_space=pltpu.VMEM)
    hbm = pl.BlockSpec(memory_space=pl.ANY)
    dma = pltpu.SemaphoreType.DMA
    new_feats, pos_out = pl.pallas_call(
        kernel,
        out_shape=(
            pltpu.VMEM((FR, NB * L, H), BF),
            pltpu.VMEM((3, FR, NB * L), F32),
        ),
        in_specs=[pl.BlockSpec(memory_space=pltpu.SMEM)] + [vmem] * 11 + [hbm] * 2,
        out_specs=(vmem, vmem),
        scratch_shapes=[
            pltpu.VMEM((FR, EXT, L, H), BF),
            pltpu.VMEM((2, G, FR, L, H), BF),
            pltpu.VMEM((2, G, FR, 128), F32),
            pltpu.VMEM((EXT, FR, 128), F32),
            pltpu.VMEM((NB * FR, 128), F32),
            pltpu.VMEM((FR * S, 128), F32),
            pltpu.VMEM((FR * S, 128), F32),
            pltpu.VMEM((FR * L, H), F32),
            pltpu.VMEM((PAIRS, 2, L, FR, H), BF),
            pltpu.VMEM((PAIRS, 2, 8, T, H), BF),
            pltpu.VMEM((PAIRS, 2, 8, 64, H), BF),
            pltpu.VMEM((PAIRS, 2, 4, 8, FR, H), BF),
            pltpu.VMEM((2, K, H, H), BF),
            pltpu.VMEM((16 * T, H), F32),
            pltpu.VMEM((16 * T, H), F32),
            pltpu.VMEM((FR * L, H), F32),
            pltpu.VMEM((4, 2 * H, 2 * H), BF),
            pltpu.VMEM((2 * H, 2 * H), BF),
            pltpu.VMEM((2 * H, 2 * H), BF),
            pltpu.VMEM((4, 2 * H, H), BF),
            pltpu.VMEM((H, H), BF),
            pltpu.VMEM((H, H), BF),
            dma((2,)),
            dma((2,)),
            dma((2,)),
            dma((2, G)),
            dma((2, G)),
            dma((PAIRS, 2, 7)),
            dma((PAIRS, 2, 7)),
            dma((PAIRS, 2, 3)),
            dma((PAIRS, 2, 3)),
        ],
        compiler_params=pltpu.CompilerParams(
            collective_id=0, has_side_effects=True, vmem_limit_bytes=56 * 1024 * 1024
        ),
    )(
        idx,
        pos3,
        edge_in,
        edge_out,
        edge_params,
        coord_weight.reshape(1, H),
        node_in,
        node_out,
        node_bias,
        fwd,
        inv_hi,
        inv_lo,
        node_feats.reshape(FR, NB, L, H),
        spectral,
    )
    new_positions = jnp.transpose(pos_out, (1, 0, 2))
    return (new_feats, new_positions)


def solution(mesh):
    placed = (
        P("tm", "space", None),
        P("tm", None, "space"),
        P("tm", "space", None),
        P(),
        P(),
        P(),
        P(),
        P(),
        P(),
        P(),
        P(),
    )
    return jax.shard_map(
        shards,
        mesh=mesh,
        in_specs=placed,
        out_specs=(P("tm", "space", None), P("tm", None, "space")),
        check_vma=False,
    )
```
